32 devices in a mesh: rep: 4 (over z), fsdp: 4 (over x, core), ctx: 2 (over y).
Axes of the slice: x: 2, y: 2, z: 4, core: 2. Of those that a mesh axis runs over, the one named last changes fastest.
Arguments:
- residual_in: bfloat16 [16, 1024, 1024], P(('rep', 'fsdp'), 'ctx'), may hold values from -6 to 6
- block_order: int32 [16, 4], P(('rep', 'fsdp')), may hold values from 0 to 3, each once within a row
- ln1_gain: bfloat16 [1024], P('fsdp'), may hold values from 0.25 to 1.75
- ln1_bias: bfloat16 [1024], P('fsdp'), may hold values from -4 to 4
- ln2_gain: bfloat16 [1024], P('fsdp'), may hold values from 0.25 to 1.75
- ln2_bias: bfloat16 [1024], P('fsdp'), may hold values from -4 to 4
- w_qkv: bfloat16 [1024, 3072], P('fsdp'), may hold values from -0.1875 to 0.1875
- b_qkv: bfloat16 [3072], P('fsdp'), may hold values from -4 to 4
- w_out: bfloat16 [1024, 1024], P('fsdp'), may hold values from -0.75 to 0.75
- b_out: bfloat16 [1024], P('fsdp'), may hold values from -4 to 4
- w_up: bfloat16 [1024, 4096], P('fsdp'), may hold values from -0.1875 to 0.1875
- b_up: bfloat16 [4096], P('fsdp'), may hold values from -6 to 6
- w_down: bfloat16 [4096, 1024], P('fsdp'), may hold values from -0.09375 to 0.09375
- b_down: bfloat16 [1024], P('fsdp'), may hold values from -4 to 4
- cotangent: bfloat16 [16, 1024, 1024], P(('rep', 'fsdp'), 'ctx'), may hold values from -6 to 6
Outputs:
- out: bfloat16 [16, 1024, 1024], P(('rep', 'fsdp'), 'ctx')
- grad_input: float32 [16, 1024, 1024], P(('rep', 'fsdp'), 'ctx')
- grad_ln1_gain: float32 [1024], P('fsdp')
- grad_ln1_bias: float32 [1024], P('fsdp')
- grad_ln2_gain: float32 [1024], P('fsdp')
- grad_ln2_bias: float32 [1024], P('fsdp')
- grad_w_qkv: float32 [1024, 3072], P('fsdp')
- grad_b_qkv: float32 [3072], P('fsdp')
- grad_w_out: float32 [1024, 1024], P('fsdp')
- grad_b_out: float32 [1024], P('fsdp')
- grad_w_up: float32 [1024, 4096], P('fsdp')
- grad_b_up: float32 [4096], P('fsdp')
- grad_w_down: float32 [4096, 1024], P('fsdp')
- grad_b_down: float32 [1024], P('fsdp')
The draws below stay inside these ranges and needn't reach their ends.
Inputs may be any that keep to these rules, and one draw needn't show every extreme that they name: Each row is a permutation of the block numbers of one sequence; block slot b (storage slots b * 256 to (b + 1) * 256 - 1) holds the sequence's block block_order[s, b].
All inputs are finite; a program needn't handle non-finite values.
Results may differ from the reference program's by a relative error of at most 0.01.
Values may be sent and summed in bfloat16 or wider, within the bound.
A program may use at most 192 MiB of HBM per device.

```python
import math
import jax
import jax.numpy as jnp
from jax import lax

D = 1024
HEADS = 16
HEAD = 64
ROT = 16
FF = 4096
BLK = 256
SEQ_LEN = 1024
SEQUENCES = 16
N_CTX = 2


def shard_levels(key, dims, pieces, smallest, top_value):
    def one(dim, parts):
        steps = jax.random.uniform(jax.random.fold_in(jax.random.fold_in(key, 6), dim), (parts,), jnp.float32, smallest / len(pieces), top_value / len(pieces))
        return jnp.repeat(jnp.exp(steps), dims[dim] // parts).reshape((-1,) + (1,) * (len(dims) - dim - 1))

    level = one(*pieces[0])
    for cut in pieces[1:]:
        level = level * one(*cut)
    return level


def normal_values(stream_key, dims, deviation, limit, shards=(), kind=jnp.bfloat16):
    drawn = deviation * jax.random.normal(stream_key, dims, jnp.float32)
    if shards:
        drawn = drawn * shard_levels(stream_key, dims, shards, -0.22, 0.18)
    return jnp.clip(drawn, -limit, limit).astype(kind)


def setup_inputs(seed: int = 0) -> dict:
    key_list = jax.random.split(jax.random.key(seed), 16)
    return {
        "residual_in": normal_values(key_list[0], (SEQUENCES, SEQ_LEN, D), 1.0, 6.0, ((0, 16), (1, 2))),
        "block_order": jax.vmap(lambda own: jax.random.permutation(own, 2 * N_CTX))(jax.random.split(key_list[1], SEQUENCES)).reshape((SEQUENCES, 2 * N_CTX)).astype(jnp.int32),
        "ln1_gain": jnp.clip(1.0 + 0.15 * jax.random.normal(key_list[2], (D,), jnp.float32), 0.25, 1.75).astype(jnp.bfloat16),
        "ln1_bias": normal_values(key_list[3], (D,), 0.3, 4.0, ((0, 4),)),
        "ln2_gain": jnp.clip(1.0 + 0.15 * jax.random.normal(key_list[4], (D,), jnp.float32), 0.25, 1.75).astype(jnp.bfloat16),
        "ln2_bias": normal_values(key_list[5], (D,), 0.3, 4.0, ((0, 4),)),
        "w_qkv": normal_values(key_list[6], (D, 3 * D), D ** -0.5, 0.1875, ((0, 4),)),
        "b_qkv": normal_values(key_list[7], (3 * D,), 0.3, 4.0, ((0, 4),)),
        "w_out": normal_values(key_list[8], (D, D), (D // 16) ** -0.5, 0.75, ((0, 4),)),
        "b_out": normal_values(key_list[9], (D,), 0.3, 4.0, ((0, 4),)),
        "w_up": normal_values(key_list[10], (D, FF), D ** -0.5, 0.1875, ((0, 4),)),
        "b_up": normal_values(key_list[11], (FF,), 0.5, 6.0, ((0, 4),)),
        "w_down": normal_values(key_list[12], (FF, D), FF ** -0.5, 0.09375, ((0, 4),)),
        "b_down": normal_values(key_list[13], (D,), 0.3, 4.0, ((0, 4),)),
        "cotangent": normal_values(key_list[14], (SEQUENCES, SEQ_LEN, D), 1.0, 6.0, ((0, 16), (1, 2))),
    }


@jax.custom_vjp
def low(v):
    return lax.optimization_barrier(v.astype(jnp.bfloat16)).astype(jnp.float32)

@jax.custom_vjp
def low_back(v):
    return v

def low_keep(v):
    return (low(v), None)

def low_pass(kept, grad):
    return (grad,)

def back_keep(v):
    return (v, None)

def back_low(kept, grad):
    return (low(grad),)
low.defvjp(low_keep, low_pass)
low_back.defvjp(back_keep, back_low)
precise = lax.Precision.HIGHEST

def layer_norm(values, gain_vec, bias_vec):
    center = values - lax.optimization_barrier(jnp.mean(values, -1, keepdims=True))
    spread = lax.optimization_barrier(jnp.mean(center * center, -1, keepdims=True))
    return center * lax.rsqrt(spread + 1e-05) * gain_vec + bias_vec

def rotary_tables(positions):
    halves = ROT // 2
    inverse = 10000.0 ** (-(2.0 * jnp.arange(halves, dtype=jnp.float32)) / ROT)
    angles = positions.astype(jnp.float32)[:, None] * inverse[None, :]
    return (jnp.cos(angles)[:, None, :], jnp.sin(angles)[:, None, :])

def turn(values, cosine, sine_tab):
    halves = ROT // 2
    first_half = values[..., :halves]
    second_half = values[..., halves:ROT]
    return jnp.concatenate([first_half * cosine - second_half * sine_tab, second_half * cosine + first_half * sine_tab, values[..., ROT:]], -1)

def forward(tokens, params, positions):
    gain_one, bias_one, gain_two, bias_two, w_qkv, b_qkv, w_out, b_out, w_up, b_up, w_down, b_down = params
    length = tokens.shape[0]
    normed_one = low(layer_norm(tokens, gain_one, bias_one))
    projected = low_back(jnp.dot(normed_one, w_qkv, precision=precise) + b_qkv)
    cosine, sine_tab = rotary_tables(positions)
    queries = low(turn(projected[:, :D].reshape(length, HEADS, HEAD), cosine, sine_tab))
    keys_all = low(turn(projected[:, D:2 * D].reshape(length, HEADS, HEAD), cosine, sine_tab))
    values_all = low(projected[:, 2 * D:].reshape(length, HEADS, HEAD))
    rows_step = min(length, 512)
    blocks = length // rows_step
    factor = 1.0 / math.sqrt(HEAD)

    def attend(block_item):
        query_blk, query_pos = block_item
        scores = jnp.einsum('qhd,khd->hqk', query_blk, keys_all, precision=precise) * factor
        scores = low_back(scores)
        allowed = positions[None, None, :] <= query_pos[None, :, None]
        scores = jnp.where(allowed, scores, -1e+30)
        row_max = lax.optimization_barrier(jnp.max(scores, -1, keepdims=True))
        weights = jnp.exp(scores - row_max)
        weights = weights / lax.optimization_barrier(jnp.sum(weights, -1, keepdims=True))
        return jnp.einsum('hqk,khd->qhd', low(weights), values_all, precision=precise)
    mixed_heads = lax.map(jax.checkpoint(attend), (queries.reshape(blocks, rows_step, HEADS, HEAD), positions.reshape(blocks, rows_step)))
    context = low_back(low(mixed_heads.reshape(length, D)))
    attention = jnp.dot(context, w_out, precision=precise) + b_out
    normed_two = low(layer_norm(tokens, gain_two, bias_two))
    hidden_pre = low_back(jnp.dot(normed_two, w_up, precision=precise) + b_up)
    hidden = low(jax.nn.gelu(hidden_pre, approximate=False))
    feed_out = jnp.dot(hidden, w_down, precision=precise) + b_down
    return tokens + attention + feed_out

def reference(residual_in, block_order, ln1_gain, ln1_bias, ln2_gain, ln2_bias, w_qkv, b_qkv, w_out, b_out, w_up, b_up, w_down, b_down, cotangent):
    params = tuple((p_item.astype(jnp.float32) for p_item in (ln1_gain, ln1_bias, ln2_gain, ln2_bias, w_qkv, b_qkv, w_out, b_out, w_up, b_up, w_down, b_down)))
    slot_ids = jnp.arange(SEQ_LEN, dtype=jnp.int32)

    def one_sequence(grad_total, seq_item):
        seq_tokens, seq_order, seq_cot = seq_item
        positions = (seq_order[slot_ids // BLK] * BLK + slot_ids % BLK).astype(jnp.int32)

        def run_layer(tok_values, param_values):
            return forward(tok_values, param_values, positions)
        result, pull_back = jax.vjp(run_layer, seq_tokens.astype(jnp.float32), params)
        grad_tokens, grad_params = pull_back(seq_cot.astype(jnp.float32))
        grad_total = tuple((acc_item + new_item for acc_item, new_item in zip(grad_total, grad_params)))
        return (grad_total, (result.astype(jnp.bfloat16), grad_tokens))
    zero_grads = tuple((jnp.zeros(p_item.shape, jnp.float32) for p_item in params))
    grads, (outputs, grads_in) = lax.scan(one_sequence, zero_grads, (residual_in, block_order, cotangent))
    return (outputs, grads_in, grads[0], grads[1], grads[2], grads[3], grads[4], grads[5], grads[6], grads[7], grads[8], grads[9], grads[10], grads[11])
```

```python
import functools
import math

import jax
import jax.numpy as jnp
from jax import lax
from jax.experimental import pallas as pl
from jax.experimental.pallas import tpu as pltpu
from jax.sharding import PartitionSpec as P

HEADS = 16
HEAD = 64
ROT = 16
BLK = 256
EPSILON = 1e-05
CW = 512
HW = CW // 2
TT = 256
SLOTS = 4
LINK = pl.DeviceIdType.MESH
BF = jnp.bfloat16
F32 = jnp.float32

NN = (((1,), (0,)), ((), ()))
NT = (((1,), (1,)), ((), ()))
TN = (((0,), (0,)), ((), ()))


def mm(a, b, dims=NN):
    return lax.dot_general(a, b, dims, preferred_element_type=F32)


def mult(value, of):
    return value if isinstance(value, int) else pl.multiple_of(value, of)


def kernel(
    dims,
    x_ref,
    g_ref,
    oh_ref,
    sm_ref,
    wqkv_ref,
    wo_ref,
    wup_ref,
    wdn_ref,
    tab_ref,
    fin_up,
    fin_dn,
    fin_qkv,
    fin_o,
    out_ref,
    gin_ref,
    sg_ref,
    gbuf,
    xrecv,
    ar,
    af,
    mo,
    X3,
    G3,
    wup,
    wdn,
    wqkv,
    wo,
    oh_v,
    sm_v,
    vecs,
    sgv,
    sgA,
    sgB,
    own,
    yrecv,
    zin,
    zback,
    ysend,
    st,
    tot,
    sems,
):
    X, NREP, R, D, FF = dims
    L = 2 * R
    RX = D // X
    RS = D // (2 * X)
    SW = CW // X
    NJ = FF // 2 // CW
    NB = L // TT
    NP = 2 * NJ + 4
    h = NREP // 2

    f = lax.axis_index("fsdp")
    y = lax.axis_index("ctx")
    r = lax.axis_index("rep")
    c = lax.rem(f, 2)
    xi = lax.div(f, 2)
    fs = xi * 2 + (1 - c)
    yo = 1 - y

    counter = [0]

    def S():
        counter[0] += 1
        return counter[0] - 1

    def rcopy(src, dst, ss, rs, **dev):
        cp = pltpu.make_async_remote_copy(
            src_ref=src,
            dst_ref=dst,
            send_sem=sems.at[ss],
            recv_sem=sems.at[rs],
            device_id=dev,
            device_id_type=LINK,
        )
        cp.start()
        return cp

    def lcopy(src, dst, s):
        cp = pltpu.make_async_copy(src, dst, sems.at[s])
        cp.start()
        return cp

    def wait(s, ref):
        pltpu.make_async_copy(ref, ref, sems.at[s]).wait()

    finals = []

    NG = NJ + 2
    gxs = [S() for _ in range(NG)]
    gxr = [S() for _ in range(NG)]
    gzs = [S() for _ in range(NG)]
    gzr = [S() for _ in range(NG)]
    gcs = [S() for _ in range(NG)]
    gcr = [S() for _ in range(NG)]
    gl = [S() for _ in range(NG)]
    q = lax.rem(r, 2)
    zp = r + 1 - 2 * q

    def cols(k, ct):
        if k < NJ:
            for xx in range(X):
                yield (
                    wup_ref,
                    mult((FF // X) * xx + (FF // (2 * X)) * ct + SW * k, 128),
                    wup.at[k],
                    xx * SW,
                )
        elif k == NJ:
            for m in range(3):
                for xx in range(X):
                    yield (
                        wqkv_ref,
                        mult(D * m + (D // X) * xx + SW * ct, 128),
                        wqkv,
                        m * CW + xx * SW,
                    )

    def rows_of(k):
        if k < NJ:
            return (wdn_ref, SW * k, wdn.at[k])
        if k == NJ + 1:
            return (wo_ref, 0, wo)
        return None

    def part(ref, row, n, col, w):
        return ref.at[pl.ds(row, n), pl.ds(col, w)]

    def span(ref, row, n):
        return ref.at[pl.ds(row, n)]

    def xz_bytes(k):
        if k < NJ:
            return gbuf.at[0, pl.ds(0, X - 1)]
        if k == NJ:
            return xrecv.at[pl.ds(0, 3), :, pl.ds(0, RX // 2)]
        return gbuf.at[0, pl.ds(0, X - 1), pl.ds(0, RX // 2)]

    def gather_x(k):
        n = RS // 2
        r0 = mult(q * n, n)
        for dx in range(1, X):
            xo = lax.rem(xi + dx, X)
            for ct in range(2):
                for src, sc, dst, dc in cols(k, ct):
                    rcopy(
                        part(src, r0, n, sc, SW),
                        part(dst, mult(RS * f + r0, n), n, dc, SW),
                        gxs[k],
                        gxr[k],
                        fsdp=2 * xo + ct,
                    )
            rw = rows_of(k)
            if rw is not None:
                src, sr, dst = rw
                rcopy(
                    span(src, mult(sr + r0, n), n),
                    span(dst, mult(xi * SW + r0, n), n),
                    gxs[k],
                    gxr[k],
                    fsdp=2 * xo + c,
                )
        finals.append(lambda: wait(gxs[k], xz_bytes(k)))

    def gather_fwd(k):
        wait(gxr[k], xz_bytes(k))
        n = RS // 2
        r0 = mult(q * n, n)
        dst = wup.at[k] if k < NJ else wqkv
        for dx in range(1, X):
            xo = lax.rem(xi + dx, X)
            if k <= NJ:
                for ct in range(2):
                    piece = span(dst, mult(RS * (2 * xo + ct) + r0, n), n)
                    rcopy(piece, piece, gzs[k], gzr[k], rep=zp)
            rw = rows_of(k)
            if rw is not None:
                piece = span(rw[2], mult(xo * SW + r0, n), n)
                rcopy(piece, piece, gzs[k], gzr[k], rep=zp)
        finals.append(lambda: wait(gzs[k], xz_bytes(k)))

    def core_bytes(k):
        if k < NJ:
            return gbuf.at[0, 0, pl.ds(0, RX // 2)]
        return gbuf.at[pl.ds(0, 3), 0, pl.ds(0, RX // 2)]

    def local_bytes(k):
        n = 2 if k == NJ + 1 else 3
        return gbuf.at[pl.ds(0, n), 0, pl.ds(0, RX // 2)]

    def gather_core(k):
        for src, sc, dst, dc in cols(k, 1 - c):
            rcopy(
                part(src, 0, RS, sc, SW),
                part(dst, mult(RS * f, RS), RS, dc, SW),
                gcs[k],
                gcr[k],
                fsdp=fs,
            )
        for src, sc, dst, dc in cols(k, c):
            lcopy(part(src, 0, RS, sc, SW), part(dst, mult(RS * f, RS), RS, dc, SW), gl[k])
        rw = rows_of(k)
        if rw is not None:
            src, sr, dst = rw
            lcopy(span(src, sr, SW), span(dst, mult(xi * SW, SW), SW), gl[k])
        if k <= NJ:
            finals.append(lambda: wait(gcs[k], core_bytes(k)))

    def gather_wait(k):
        wait(gl[k], local_bytes(k))
        if k <= NJ:
            wait(gcr[k], core_bytes(k))
        wait(gzr[k], xz_bytes(k))

    xs = [S() for _ in range(NP)]
    xr = [S() for _ in range(NP)]
    ys = [S() for _ in range(NP)]
    yr = [S() for _ in range(NP)]
    zis = [S() for _ in range(NP)]
    zir = [S() for _ in range(NP)]
    zbs = [S() for _ in range(NP)]
    zbr = [S() for _ in range(NP)]
    ags = [S() for _ in range(NP)]
    agr = [S() for _ in range(NP)]
    agl = [S() for _ in range(NP)]
    stl = S()
    lp = S()
    m = jnp.where(r < h, r, NREP - 1 - r)
    inner = jnp.where(r < h, r + 1, r - 1)
    outer = jnp.where(r < h, r - 1, r + 1)

    def is_up(p):
        return (p < 2 * NJ and p % 2 == 0) or p > 2 * NJ

    def x_bytes():
        return gbuf.at[0, pl.ds(0, X - 1)]

    def send_x(p):
        for dx in range(1, X):
            xo = lax.rem(xi + dx, X)
            rcopy(gbuf.at[p, xo], xrecv.at[p, dx - 1], xs[p], xr[p], fsdp=2 * xo + c)
        finals.append(lambda: wait(xs[p], x_bytes()))

    def add_rows(count, fn):
        def step(i, carry):
            fn(pl.ds(mult(i * 64, 64), 64))
            return carry

        lax.fori_loop(0, count // 64, step, 0)

    def stage_x(p):
        wait(xr[p], x_bytes())
        for side, half in ((0, yo), (1, y)):
            at = pl.ds(mult(half * HW, HW), HW)
            lcopy(gbuf.at[p, xi, :, at], st.at[side], stl)
            for d in range(X - 1):
                lcopy(xrecv.at[p, d, :, at], st.at[2 + 2 * d + side], stl)
        slot = p % SLOTS
        if p >= SLOTS:
            wait(ys[p - SLOTS], ysend.at[0])
        wait(stl, gbuf.at[0])

        def add(rows):
            for side in range(2):
                total = st[side, rows, :].astype(F32)
                for d in range(X - 1):
                    total = total + st[2 + 2 * d + side, rows, :].astype(F32)
                if side == 0:
                    ysend[slot, rows, :] = total.astype(BF)
                else:
                    own[p, rows, :] = total.astype(BF)

        add_rows(RX, add)
        rcopy(ysend.at[slot], yrecv.at[p], ys[p], yr[p], ctx=yo)

    def send_in(p, at_middle):
        if at_middle:
            rcopy(own.at[p], zback.at[p], zis[p], zbr[p], rep=inner)
        else:
            rcopy(own.at[p], zin.at[p], zis[p], zir[p], rep=inner)

    def add_into(p, dst, other):
        def add(rows):
            dst[p, rows, :] = (own[p, rows, :].astype(F32) + other[p, rows, :].astype(F32)).astype(
                BF
            )

        add_rows(RX, add)

    def stage_y(p):
        wait(yr[p], own.at[0])
        add_into(p, own, yrecv)

        @pl.when(m == 0)
        def _():
            send_in(p, h == 1)

        finals.append(lambda: wait(zis[p], own.at[0]))

    def stage_in(k, p):
        @pl.when(m == k)
        def _():
            wait(zir[p], own.at[0])
            add_into(p, own, zin)
            send_in(p, k == h - 1)

    def stage_out(i, p):
        @pl.when(m == h - 1 - i)
        def _():
            wait(zbr[p], own.at[0])
            if i == 0:
                add_into(p, zback, zback)
            if h - 1 - i > 0:
                rcopy(zback.at[p], zback.at[p], zbs[p], zbr[p], rep=outer)

    def ag_bytes(p):
        return own.at[pl.ds(0, 3), pl.ds(0, RS)] if is_up(p) else own.at[0]

    def stage_ag(p):
        for i in range(X // 2):
            b = y * (X // 2) + i
            lanes = pl.ds(i * SW, SW)
            if is_up(p):
                if p < 2 * NJ:
                    dst, base, whole = fin_up, SW * (p // 2), FF
                else:
                    dst, base, whole = fin_qkv, D * (p - 2 * NJ - 1), D
                at = mult(base + (whole // X) * b + (whole // (2 * X)) * c, 128)
                mine = zback.at[p, pl.ds(mult(c * RS, RS), RS), lanes]
                theirs = zback.at[p, pl.ds(mult((1 - c) * RS, RS), RS), lanes]
                to = dst.at[:, pl.ds(at, SW)]
                lcopy(mine, to, agl[p])
                rcopy(theirs, to, ags[p], agr[p], fsdp=fs)
                rcopy(mine, to, ags[p], agr[p], ctx=yo)
                rcopy(theirs, to, ags[p], agr[p], fsdp=fs, ctx=yo)
            else:
                dst, base = (fin_dn, SW * (p // 2)) if p < 2 * NJ else (fin_o, 0)
                src = zback.at[p, :, lanes]
                to = dst.at[pl.ds(mult(b * RX, RX), RX), pl.ds(base, SW)]
                lcopy(src, to, agl[p])
                rcopy(src, to, ags[p], agr[p], ctx=yo)
        finals.append(lambda: wait(agl[p], own.at[0, pl.ds(0, RS)] if is_up(p) else own.at[0]))
        finals.append(lambda: wait(ags[p], ag_bytes(p)))
        finals.append(lambda: wait(agr[p], ag_bytes(p)))

    stages = [stage_x, stage_y]
    for k in range(1, h):
        stages.append(functools.partial(stage_in, k))
    for i in range(h):
        stages.append(functools.partial(stage_out, i))
    stages.append(stage_ag)
    live = []
    waiting = []

    def tick():
        for item in list(live):
            p, s = item
            stages[s](p)
            if s == len(stages) - 2:
                stages[s + 1](p)
                live.remove(item)
            else:
                item[1] = s + 1
        if waiting:
            p = waiting.pop(0)
            stages[0](p)
            live.append([p, 1])

    def grad_piece(p, lhs_t, rhs, gst):
        per = RX // TT

        def step(t, carry):
            b = lax.div(t, per)
            row = pl.ds(mult(lax.rem(t, per) * TT, TT), TT)
            res = mm(lhs_t[pl.ds(mult(t * TT, TT), TT), :], rhs()).astype(BF)
            if is_up(p):
                gst[b, row, :] = res
            else:
                for xx in range(X):
                    gst[xx, row, pl.ds(mult(b * SW, 128), SW)] = res[:, xx * SW : (xx + 1) * SW]
            return carry

        lax.fori_loop(0, D // TT, step, 0)
        lcopy(gst, gbuf.at[p], lp).wait()
        send_x(p)
        waiting.append(p)

    bar = pltpu.get_barrier_semaphore()
    near = []
    for df in range(2 * X):
        for dy in range(2):
            if df or dy:
                near.append(dict(fsdp=lax.rem(f + df, 2 * X), ctx=lax.rem(y + dy, 2)))
    for dr in range(1, NREP):
        near.append(dict(rep=lax.rem(r + dr, NREP)))
    for dev in near:
        pl.semaphore_signal(bar, inc=1, device_id=dev, device_id_type=LINK)
    pl.semaphore_wait(bar, len(near))

    gather_core(0)
    gather_x(0)
    s_sm, r_sm, l_sm = S(), S(), S()
    lcopy(sm_ref, sm_v.at[f], l_sm)
    for df in range(1, 2 * X):
        rcopy(sm_ref, sm_v.at[f], s_sm, r_sm, fsdp=lax.rem(f + df, 2 * X))
    s_bo, r_bo, l_bo = S(), S(), S()
    lcopy(oh_ref, oh_v.at[c], l_bo)
    rcopy(oh_ref, oh_v.at[c], s_bo, r_bo, fsdp=fs)
    tok = []
    for src, dst in ((x_ref, X3), (g_ref, G3)):
        ids = [S() for _ in range(7)]
        lcopy(src, dst.at[c], ids[0])
        rcopy(src, dst.at[c], ids[1], ids[2], fsdp=fs)
        tok.append((src, dst, ids))
    gather_x(1)
    for src, dst, ids in tok:

        @pl.when(c != y)
        def _():
            rcopy(src, dst.at[2], ids[3], ids[4], ctx=yo)

    for k in range(1, NG):
        gather_core(k)

    def exchange_forward():
        for src, dst, ids in tok:

            @pl.when(c == y)
            def _():
                wait(ids[4], dst.at[2])
                rcopy(dst.at[2], dst.at[2], ids[5], ids[6], fsdp=fs)

    def exchange_finish():
        for src, dst, ids in tok:

            @pl.when(c != y)
            def _():
                wait(ids[6], dst.at[2])
                wait(ids[3], src)

            @pl.when(c == y)
            def _():
                wait(ids[5], dst.at[2])

    wait(l_sm, sm_ref)
    wait(r_sm, sm_v.at[pl.ds(0, 2 * X - 1)])
    for ff in range(2 * X):
        vecs[:, ff * RS : (ff + 1) * RS] = sm_v[ff]
    sgv[...] = jnp.zeros_like(sgv)
    for src, dst, ids in tok:
        wait(ids[0], dst.at[0])
        wait(ids[2], dst.at[0])

    def vec(row):
        return vecs[row : row + 1, :]

    def center(blk):
        v = blk.astype(F32)
        mid = v - jnp.mean(v, -1, keepdims=True)
        rs = lax.rsqrt(jnp.mean(mid * mid, -1, keepdims=True) + EPSILON)
        return mid * rs, rs

    def norm_back(e, blk, gain, row):
        n, rs = center(blk)
        sgv[row : row + 1, :] += jnp.sum(e * n, 0, keepdims=True)
        sgv[row + 1 : row + 2, :] += jnp.sum(e, 0, keepdims=True)
        eg = e * gain
        return rs * (
            eg - jnp.mean(eg, -1, keepdims=True) - n * jnp.mean(eg * n, -1, keepdims=True)
        )

    def ds(i, size=TT):
        return pl.ds(mult(i * size, size), size)

    s_mo = [S() for _ in range(2)]
    r_mo = [S() for _ in range(2)]

    def feed(n2, n2t, gt, acc_o, acc_g, hid, gup, gst):
        def prep(b, carry):
            half, row = lax.div(b, NB // 2), ds(lax.rem(b, NB // 2))
            n, _ = center(X3[half, row, :])
            v = (n * vec(2) + vec(3)).astype(BF)
            n2[ds(b), :] = v
            n2t[:, ds(b)] = v.T
            gt[:, ds(b)] = G3[half, row, :].T
            return carry

        lax.fori_loop(0, NB, prep, 0)

        def gsum(b, carry):
            sgv[4:5, :] += jnp.sum(G3[c, ds(b), :].astype(F32), 0, keepdims=True)
            return carry

        lax.fori_loop(0, NB // 2, gsum, 0)
        gather_fwd(0)
        gather_x(2)
        gather_fwd(1)
        gather_x(3)
        exchange_forward()
        for j in range(NJ):
            gather_wait(j)
            bias = jnp.concatenate(
                [vecs[8 + j : 9 + j, ds(2 * xx + c, RS)] for xx in range(X)], 1
            )

            def tile(t, gb):
                half, row = lax.div(t, NB // 2), ds(lax.rem(t, NB // 2))
                g = G3[half, row, :]
                up = mm(n2[ds(t), :], wup[j]) + bias
                cdf = 0.5 + 0.5 * lax.erf(up * (1.0 / math.sqrt(2.0)))
                hd = (up * cdf).astype(BF)
                hid[ds(t), :] = hd
                gh = mm(g, wdn[j], NT)
                pdf = jnp.exp(-0.5 * up * up) * (1.0 / math.sqrt(2.0 * math.pi))
                gu = (gh * (cdf + up * pdf)).astype(BF)
                gup[ds(t), :] = gu
                o = mm(hd, wdn[j])
                gn = mm(gu, wup[j], NT)
                if j == 0:
                    acc_o[ds(t), :] = o
                    acc_g[ds(t), :] = gn
                else:
                    acc_o[ds(t), :] += o
                    acc_g[ds(t), :] += gn
                return gb + jnp.sum(gu.astype(F32), 0, keepdims=True)

            gb = lax.fori_loop(0, NB, tile, jnp.zeros((1, CW), F32))
            for xx in range(X):
                sgv[5 + j : 6 + j, ds(2 * xx + c, RS)] = gb[:, xx * SW : (xx + 1) * SW]
            grad_piece(2 * j, n2t, lambda: gup[...], gst)
            grad_piece(2 * j + 1, gt, lambda: hid[...], gst)
            if j + 2 < NG:
                gather_fwd(j + 2)
            if j + 4 < NG:
                gather_x(j + 4)

        def give(i, carry):
            b = (1 - c) * (NB // 2) + i
            n2[ds(i), :] = acc_o[ds(b), :].astype(BF)
            e = norm_back(acc_g[ds(b), :], X3[1 - c, ds(i), :], vec(2), 2)
            n2[ds(i + NB // 2), :] = e.astype(BF)
            return carry

        lax.fori_loop(0, NB // 2, give, 0)
        sends = [rcopy(n2.at[pl.ds(a * R, R)], mo.at[a], s_mo[a], r_mo[a], fsdp=fs) for a in range(2)]

        def keep(i, carry):
            b = c * (NB // 2) + i
            xb = X3[c, ds(i), :]
            o = acc_o[ds(b), :] + xb.astype(F32) + vec(7) + vec(12)
            tot[0, ds(i), :] = o.astype(BF)
            e = norm_back(acc_g[ds(b), :], xb, vec(2), 2)
            tot[1, ds(i), :] = (e + G3[c, ds(i), :].astype(F32)).astype(BF)
            return carry

        lax.fori_loop(0, NB // 2, keep, 0)
        for cp in sends:
            cp.wait_send()

    pl.run_scoped(
        feed,
        pltpu.VMEM((L, D), BF),
        pltpu.VMEM((D, L), BF),
        pltpu.VMEM((D, L), BF),
        pltpu.VMEM((L, D), F32),
        pltpu.VMEM((L, D), F32),
        pltpu.VMEM((L, CW), BF),
        pltpu.VMEM((L, CW), BF),
        pltpu.VMEM((X, RX, CW), BF),
    )

    s_ar = [S() for _ in range(2)]
    r_ar = [S() for _ in range(2)]
    s_af = [S() for _ in range(2)]
    r_af = [S() for _ in range(2)]
    l_af = [S() for _ in range(2)]
    l_tab, l_st = S(), S()

    def attend(n1, n1t, gs, gst_t, qkv, ctx, gctx, gproj, dkv, tab, gst, stage):
        lcopy(tab_ref, tab, l_tab)
        wait(l_bo, oh_ref)
        wait(r_bo, oh_ref)
        exchange_finish()

        def weight(b, s, width):
            w = oh_v[y, pl.ds(b * NB + s, 1), :].astype(BF)
            return jnp.concatenate([w] * (width // 128), 1)

        def place(s):
            half = s // (NB // 2) if isinstance(s, int) else lax.div(s, NB // 2)
            row = s % (NB // 2) if isinstance(s, int) else lax.rem(s, NB // 2)
            return jnp.where(half == y, y, 2), ds(row)

        def in_order(ref, b):
            total = None
            for s in range(NB):
                src, row = place(s)
                term = ref[src, row, :] * weight(b, s, D)
                total = term if total is None else total + term
            return total

        def in_slot(ref, s, width):
            total = None
            for b in range(NB):
                term = ref[b * TT : (b + 1) * TT, :] * weight(b, s, width)
                total = term if total is None else total + term
            return total

        def prep(b, carry):
            n, _ = center(in_order(X3, b))
            v = (n * vec(0) + vec(1)).astype(BF)
            n1[ds(b), :] = v
            n1t[:, ds(b)] = v.T
            gv = in_order(G3, b)
            gs[ds(b), :] = gv
            gst_t[:, ds(b)] = gv.T
            return carry

        lax.fori_loop(0, NB, prep, 0)
        wait(l_tab, tab_ref)
        tick()
        gather_wait(NJ)

        def turned(v, rows, sign):
            right = pltpu.roll(v, ROT // 2, 1)
            left = pltpu.roll(v, 128 - ROT // 2, 1)
            return v * tab[0, rows, :] + sign * (
                right * tab[1, rows, :] + left * tab[2, rows, :]
            )

        for mm_i in range(3):
            parts = []
            for xx in range(X):
                both = []
                for cc in range(2):
                    nb = 2 * X * mm_i + 2 * xx + cc
                    both.append(sm_v[nb // 3, 4 + nb % 3 : 5 + nb % 3, :])
                parts.append(jnp.where(c == 0, both[0], both[1]))
            bias = jnp.concatenate(parts, 1)

            def proj(t, carry):
                v = mm(n1[ds(t), :], wqkv[:, mm_i * CW : (mm_i + 1) * CW]) + bias
                if mm_i == 2:
                    qkv[2, ds(t), :] = v.astype(BF)
                else:
                    for u in range(CW // 128):
                        w = turned(v[:, u * 128 : (u + 1) * 128], ds(t), 1.0)
                        if mm_i == 0:
                            w = w * (1.0 / math.sqrt(HEAD))
                        qkv[mm_i, ds(t), u * 128 : (u + 1) * 128] = w.astype(BF)
                return carry

            lax.fori_loop(0, NB, proj, 0)
        tick()
        gather_wait(NJ + 1)

        def gcx(t, carry):
            gctx[ds(t), :] = mm(gs[ds(t), :], wo[...], NT).astype(BF)
            return carry

        lax.fori_loop(0, NB, gcx, 0)
        tick()

        low_half = lax.broadcasted_iota(jnp.int32, (1, 128), 1) < HEAD

        for hp in range(CW // 128):
            lanes = pl.ds(hp * 128, 128)
            dkv[...] = jnp.zeros_like(dkv)
            for i in range(NB):
                rows = pl.ds(i * TT, TT)
                n = (i + 1) * TT
                qb = qkv[0, rows, lanes]
                gb = gctx[rows, lanes]
                kb = qkv[1, pl.ds(0, n), lanes]
                vb = qkv[2, pl.ds(0, n), lanes]
                res = []
                for hd in range(2):
                    mask = low_half if hd == 0 else jnp.logical_not(low_half)
                    zero = jnp.zeros_like(qb)
                    s = mm(jnp.where(mask, qb, zero), kb, NT)
                    ahead = lax.broadcasted_iota(jnp.int32, (TT, n), 1) - lax.broadcasted_iota(
                        jnp.int32, (TT, n), 0
                    )
                    s = jnp.where(ahead <= i * TT, s, -1e30)
                    p = jnp.exp(s - jnp.max(s, -1, keepdims=True))
                    p = p * (1.0 / jnp.sum(p, -1, keepdims=True))
                    pb = p.astype(BF)
                    dp = mm(jnp.where(mask, gb, zero), vb, NT)
                    dsc = (p * (dp - jnp.sum(p * dp, -1, keepdims=True))).astype(BF)
                    res.append(
                        (mm(pb, vb), mm(dsc, kb), mm(dsc, qb, TN), mm(pb, gb, TN))
                    )
                both = [jnp.where(low_half, u, w) for u, w in zip(res[0], res[1])]
                ctx[rows, lanes] = both[0].astype(BF)
                dq = turned(both[1] * (1.0 / math.sqrt(HEAD)), rows, -1.0)
                gproj[rows, pl.ds(hp * 128, 128)] = dq.astype(BF)
                dkv[0, pl.ds(0, n), :] += both[2]
                dkv[1, pl.ds(0, n), :] += both[3]
            for i in range(NB):
                rows = pl.ds(i * TT, TT)
                gproj[rows, pl.ds(CW + hp * 128, 128)] = turned(dkv[0, rows, :], rows, -1.0).astype(
                    BF
                )
                gproj[rows, pl.ds(2 * CW + hp * 128, 128)] = dkv[1, rows, :].astype(BF)
            tick()

        grad_piece(2 * NJ, gst_t, lambda: ctx[...], gst)
        for mm_i in range(3):
            grad_piece(
                2 * NJ + 1 + mm_i, n1t, lambda: gproj[:, mm_i * CW : (mm_i + 1) * CW], gst
            )
        tick()

        def att_out(s, carry):
            n1[ds(s), :] = mm(in_slot(ctx, s, CW), wo[...]).astype(BF)
            return carry

        lax.fori_loop(0, NB, att_out, 0)

        def hand(a, buf):
            @pl.when(c != y)
            def _():
                rcopy(buf, ar.at[a], s_ar[a], r_ar[a], fsdp=fs)

        hand(0, n1)

        def att_in(s, carry):
            e = mm(in_slot(gproj, s, 3 * CW), wqkv[...], NT)
            src, row = place(s)
            gs[ds(s), :] = norm_back(e, X3[src, row, :], vec(0), 0).astype(BF)
            return carry

        lax.fori_loop(0, NB, att_in, 0)
        hand(1, gs)

        for mm_i in range(3):
            gb = jnp.sum(gproj[:, mm_i * CW : (mm_i + 1) * CW].astype(F32), 0, keepdims=True)
            for xx in range(X):
                for cc in range(2):
                    nb = 2 * X * mm_i + 2 * xx + cc
                    at = nb // 3

                    @pl.when(c == cc)
                    def _():
                        sgv[9 + nb % 3 : 10 + nb % 3, at * RS : (at + 1) * RS] = gb[
                            :, xx * SW : (xx + 1) * SW
                        ]

        here = f * 2 + y
        lcopy(sgv, sgA.at[here], l_sga)
        for dev in near[: 4 * X - 1]:
            rcopy(sgv, sgA.at[here], s_sga, r_sga, **dev)
        tick()

        for a, buf in ((0, n1), (1, gs)):

            @pl.when(c == y)
            def _():
                wait(r_ar[a], ar.at[a])

                def take(s, carry):
                    lcopy(ar.at[a, ds(s)], stage, l_st).wait()
                    buf[ds(s), :] = (
                        buf[ds(s), :].astype(F32) + stage[...].astype(F32)
                    ).astype(BF)
                    return carry

                lax.fori_loop(0, NB, take, 0)
                rcopy(buf.at[ds(yo, R)], af.at[a], s_af[a], r_af[a], ctx=yo)
                lcopy(buf.at[ds(y, R)], af.at[a], l_af[a])

        tick()

        for a, buf in ((0, n1), (1, gs)):

            @pl.when(c == y)
            def _():
                wait(s_af[a], af.at[a])
                wait(l_af[a], af.at[a])

            @pl.when(c != y)
            def _():
                wait(s_ar[a], ar.at[a])
                wait(r_af[a], af.at[a])

        tick()

    s_sga, r_sga, l_sga = S(), S(), S()
    s_sgb, r_sgb, l_sgb = S(), S(), S()
    pl.run_scoped(
        attend,
        pltpu.VMEM((L, D), BF),
        pltpu.VMEM((D, L), BF),
        pltpu.VMEM((L, D), BF),
        pltpu.VMEM((D, L), BF),
        pltpu.VMEM((3, L, CW), BF),
        pltpu.VMEM((L, CW), BF),
        pltpu.VMEM((L, CW), BF),
        pltpu.VMEM((L, 3 * CW), BF),
        pltpu.VMEM((2, L, 128), F32),
        pltpu.VMEM((3, L, 128), F32),
        pltpu.VMEM((X, RX, CW), BF),
        pltpu.VMEM((TT, D), BF),
    )

    def finish(s1, s2, o1, o2):
        for a in range(2):
            wait(r_mo[a], mo.at[a])
        for i in range(R // TT):
            for a, dst, stg in ((0, out_ref, o1), (1, gin_ref, o2)):
                lcopy(mo.at[a, ds(i)], s1, l_st).wait()
                lcopy(af.at[a, ds(i)], s2, l_st).wait()
                total = tot[a, ds(i), :].astype(F32) + s1[...].astype(F32) + s2[...].astype(F32)
                stg[...] = total.astype(stg.dtype)
                lcopy(stg, dst.at[ds(i)], l_st).wait()

    wait(l_sga, sgv)
    wait(r_sga, sgA.at[pl.ds(0, 4 * X - 1)])
    total = sgA[0]
    for i in range(1, 4 * X):
        total = total + sgA[i]
    wait(s_sga, sgA.at[pl.ds(0, 4 * X - 1)])
    sgv[...] = total
    lcopy(sgv, sgB.at[r], l_sgb)
    for dev in near[4 * X - 1 :]:
        rcopy(sgv, sgB.at[r], s_sgb, r_sgb, **dev)

    pl.run_scoped(
        finish,
        pltpu.VMEM((TT, D), BF),
        pltpu.VMEM((TT, D), BF),
        pltpu.VMEM((TT, D), BF),
        pltpu.VMEM((TT, D), F32),
    )
    tick()
    wait(l_sgb, sgv)
    wait(r_sgb, sgB.at[pl.ds(0, NREP - 1)])
    wait(s_sgb, sgB.at[pl.ds(0, NREP - 1)])
    total = sgB[0]
    for i in range(1, NREP):
        total = total + sgB[i]
    sgv[...] = total
    lcopy(sgv, sg_ref, l_sga).wait()

    while live or waiting:
        tick()

    wait(s_sm, sm_v.at[pl.ds(0, 2 * X - 1)])
    wait(s_bo, oh_ref)
    for src, dst, ids in tok:
        wait(ids[1], src)
    for p in range(NP - SLOTS, NP):
        wait(ys[p], ysend.at[0])
    for fn in finals:
        fn()
    if h > 1:

        @pl.when(m > 0)
        def _():
            for p in range(NP):
                wait(zbs[p], own.at[0])


def sem_count(NJ, NREP):
    return 7 * (NJ + 2) + 11 * (2 * NJ + 4) + 64


def body(
    residual_in,
    block_order,
    ln1_gain,
    ln1_bias,
    ln2_gain,
    ln2_bias,
    w_qkv,
    b_qkv,
    w_out,
    b_out,
    w_up,
    b_up,
    w_down,
    b_down,
    cotangent,
):
    R, D = residual_in.shape[1:]
    FF = w_up.shape[1]
    NF = lax.axis_size("fsdp")
    NREP = lax.axis_size("rep")
    X = NF // 2
    L, RX, RS = 2 * R, D // X, D // NF
    NJ = FF // 2 // CW
    NP = 2 * NJ + 4
    f = lax.axis_index("fsdp")

    order = block_order[0]
    count = order.shape[0]
    spots = jnp.arange(count, dtype=jnp.int32)
    where = (order[None, :] == spots[:, None]).astype(F32).reshape(-1, 1)
    where = jnp.broadcast_to(where, (count * count, 128))
    small = jnp.concatenate(
        [
            v.astype(F32).reshape(-1, RS)
            for v in (ln1_gain, ln1_bias, ln2_gain, ln2_bias, b_qkv, b_out, b_up, b_down)
        ]
        + [jnp.zeros((3, RS), F32)],
        0,
    )
    halves = ROT // 2
    lane = jnp.arange(128, dtype=jnp.int32) % HEAD
    inv = 10000.0 ** (-(2.0 * (lane % halves).astype(F32)) / ROT)
    angles = jnp.arange(L, dtype=F32)[:, None] * inv[None, :]
    turning = (lane < ROT)[None, :]
    first = (lane < halves)[None, :]
    cosine, sine = jnp.cos(angles), jnp.sin(angles)
    tab = jnp.stack(
        [
            jnp.where(turning, cosine, 1.0),
            jnp.where(turning & ~first, sine, 0.0),
            jnp.where(first, -sine, 0.0),
        ]
    )

    anywhere = pl.BlockSpec(memory_space=pl.ANY)
    sds = jax.ShapeDtypeStruct
    outs = pl.pallas_call(
        functools.partial(kernel, (X, NREP, R, D, FF)),
        out_shape=(
            sds((RS, FF), BF),
            sds((D, FF // NF), BF),
            sds((RS, 3 * D), BF),
            sds((D, RS), BF),
            sds((R, D), BF),
            sds((R, D), F32),
            sds((16, D), F32),
            sds((NP, X, RX, CW), BF),
            sds((NP, X - 1, RX, CW), BF),
            sds((2, L, D), BF),
            sds((2, R, D), BF),
            sds((2, R, D), BF),
        ),
        in_specs=[anywhere] * 9,
        out_specs=(anywhere,) * 12,
        scratch_shapes=[
            pltpu.VMEM((3, R, D), BF),
            pltpu.VMEM((3, R, D), BF),
            pltpu.VMEM((NJ, D, CW), BF),
            pltpu.VMEM((NJ, CW, D), BF),
            pltpu.VMEM((D, 3 * CW), BF),
            pltpu.VMEM((CW, D), BF),
            pltpu.VMEM((2, (L // TT) ** 2, 128), F32),
            pltpu.VMEM((NF, 16, RS), F32),
            pltpu.VMEM((16, D), F32),
            pltpu.VMEM((16, D), F32),
            pltpu.VMEM((2 * NF, 16, D), F32),
            pltpu.VMEM((NREP, 16, D), F32),
            pltpu.VMEM((NP, RX, HW), BF),
            pltpu.VMEM((NP, RX, HW), BF),
            pltpu.VMEM((NP, RX, HW), BF),
            pltpu.VMEM((NP, RX, HW), BF),
            pltpu.VMEM((SLOTS, RX, HW), BF),
            pltpu.VMEM((2 * X, RX, HW), BF),
            pltpu.VMEM((2, R, D), BF),
            pltpu.SemaphoreType.DMA((sem_count(NJ, NREP),)),
        ],
        compiler_params=pltpu.CompilerParams(
            collective_id=0, has_side_effects=True, vmem_limit_bytes=63 * 1024 * 1024
        ),
    )(
        residual_in.reshape(R, D),
        cotangent.reshape(R, D),
        where,
        small,
        w_qkv,
        w_out,
        w_up,
        w_down,
        tab,
    )
    fin_up, fin_dn, fin_qkv, fin_o, out, gin, sg = outs[:7]
    mine = lax.dynamic_slice(sg, (0, f * RS), (16, RS))
    return (
        out[None],
        gin[None],
        mine[0],
        mine[1],
        mine[2],
        mine[3],
        fin_qkv.astype(F32),
        mine[9:12].reshape(-1),
        fin_o.astype(F32).T,
        mine[4],
        fin_up.astype(F32),
        mine[5:9].reshape(-1),
        fin_dn.astype(F32).T,
        mine[4],
    )


def solution(mesh):
    in_specs = (
        P(("rep", "fsdp"), "ctx", None),
        P(("rep", "fsdp"), None),
        P("fsdp"),
        P("fsdp"),
        P("fsdp"),
        P("fsdp"),
        P("fsdp", None),
        P("fsdp"),
        P("fsdp", None),
        P("fsdp"),
        P("fsdp", None),
        P("fsdp"),
        P("fsdp", None),
        P("fsdp"),
        P(("rep", "fsdp"), "ctx", None),
    )
    out_specs = (
        P(("rep", "fsdp"), "ctx", None),
        P(("rep", "fsdp"), "ctx", None),
        P("fsdp"),
        P("fsdp"),
        P("fsdp"),
        P("fsdp"),
        P("fsdp", None),
        P("fsdp"),
        P("fsdp", None),
        P("fsdp"),
        P("fsdp", None),
        P("fsdp"),
        P("fsdp", None),
        P("fsdp"),
    )
    return jax.shard_map(body, mesh=mesh, in_specs=in_specs, out_specs=out_specs, check_vma=False)
```

```python
import functools
import math

import jax
import jax.numpy as jnp
import numpy as np
from jax import lax
from jax.experimental import pallas as pl
from jax.experimental.pallas import tpu as pltpu
from jax.sharding import PartitionSpec as P

HEADS = 16
HEAD = 64
ROT = 16
BLK = 256
EPSILON = 1e-05
PW = 256
TT = 256
FLIGHT = 4
LINK = pl.DeviceIdType.MESH
BF = jnp.bfloat16
F32 = jnp.float32

NN = (((1,), (0,)), ((), ()))
NT = (((1,), (1,)), ((), ()))
TN = (((0,), (0,)), ((), ()))


def mm(a, b, dims=NN):
    return lax.dot_general(a, b, dims, preferred_element_type=F32)


def mult(value, of):
    return value if isinstance(value, int) else pl.multiple_of(value, of)


def kernel(
    dims,
    x_ref,
    g_ref,
    oh_ref,
    sm_ref,
    wqkv_ref,
    wo_ref,
    wup_ref,
    wdn_ref,
    tab_ref,
    fin_up,
    fin_dn,
    fin_qkv,
    fin_o,
    out_ref,
    gin_ref,
    sg_ref,
    gbuf,
    mo,
    af,
    X4,
    G4,
    wup,
    wdn,
    wqkv,
    wo,
    oh_v,
    sm_v,
    vecs,
    sgv,
    sgA,
    sgB,
    own,
    zin,
    zback,
    xrecv,
    OB,
    TB,
    sems,
):
    X, NREP, R, D, FF = dims
    L = 2 * R
    T = 2 * L
    RX = D // X
    RS = D // (2 * X)
    FL = FF // 4
    HC = D // 4
    FX, HX = FL // X, HC // X
    NB = L // TT
    NU = FL // PW
    NP = 2 * NU + 4

    f = lax.axis_index("fsdp")
    y = lax.axis_index("ctx")
    r = lax.axis_index("rep")
    c = lax.rem(f, 2)
    xi = lax.div(f, 2)
    fs = xi * 2 + (1 - c)
    yo = 1 - y

    counter = [0]

    def S():
        counter[0] += 1
        return counter[0] - 1

    def rcopy(src, dst, ss, rs, **dev):
        cp = pltpu.make_async_remote_copy(
            src_ref=src,
            dst_ref=dst,
            send_sem=sems.at[ss],
            recv_sem=sems.at[rs],
            device_id=dev,
            device_id_type=LINK,
        )
        cp.start()
        return cp

    def lcopy(src, dst, s):
        cp = pltpu.make_async_copy(src, dst, sems.at[s])
        cp.start()
        return cp

    def wait(s, ref):
        pltpu.make_async_copy(ref, ref, sems.at[s]).wait()

    def ds(i, size=TT):
        return pl.ds(mult(i * size, size), size)

    finals = []

    NG = 4
    gxs = [S() for _ in range(NG)]
    gxr = [S() for _ in range(NG)]
    gzs = [S() for _ in range(NG)]
    gzr = [S() for _ in range(NG)]
    gcs = [S() for _ in range(NG)]
    gcr = [S() for _ in range(NG)]
    gl = [S() for _ in range(NG)]
    q = lax.rem(r, 2)
    zp = r + 1 - 2 * q
    dest = [wup, wdn, wqkv, wo]

    def cols(k, ct):
        if k == 0:
            for xx in range(X):
                at = (FF // X) * xx + (FF // (2 * X)) * ct + FX * y
                yield wup_ref, mult(at, 128), xx * FX, FX
        elif HX >= 128:
            for m in range(3):
                for xx in range(X):
                    at = D * m + (D // X) * xx + (D // (2 * X)) * ct + HX * y
                    yield wqkv_ref, mult(at, 128), m * HC + xx * HX, HX
        else:
            yield wqkv_ref, mult((2 * ct + y) * 3 * HC, 128), 0, 3 * HC

    def part(ref, row, n, col, w):
        return ref.at[pl.ds(row, n), pl.ds(col, w)]

    def span(ref, row, n):
        return ref.at[pl.ds(row, n)]

    def xz_bytes(k):
        if k < 2:
            return gbuf.at[pl.ds(0, 2), pl.ds(0, X - 1)]
        return gbuf.at[pl.ds(0, 3 if k == 2 else 1), pl.ds(0, X - 1), pl.ds(0, RX // 2)]

    def core_bytes(k):
        if k == 0:
            return gbuf.at[pl.ds(0, 2), 0]
        return gbuf.at[pl.ds(0, 3), 0, pl.ds(0, RX // 2)]

    def local_bytes(k):
        if k == 2:
            return core_bytes(k)
        return gbuf.at[pl.ds(0, (2, 4, 0, 1)[k]), 0]

    def rows_of(k):
        return (wdn_ref, FX) if k == 1 else (wo_ref, HX)

    def gather_x(k):
        for dx in range(1, X):
            xo = lax.rem(xi + dx, X)
            if k in (0, 2):
                n = RS // 2
                r0 = mult(q * n, n)
                for ct in range(2):
                    for src, sc, dc, w in cols(k, ct):
                        rcopy(
                            part(src, r0, n, sc, w),
                            part(dest[k], mult(RS * f + r0, n), n, dc, w),
                            gxs[k],
                            gxr[k],
                            fsdp=2 * xo + ct,
                        )
            else:
                src, w = rows_of(k)
                n = w // 2
                rcopy(
                    span(src, mult(w * y + q * n, n), n),
                    span(dest[k], mult(w * xi + q * n, n), n),
                    gxs[k],
                    gxr[k],
                    fsdp=2 * xo + c,
                )
        finals.append(lambda: wait(gxs[k], xz_bytes(k)))

    def gather_fwd(k):
        wait(gxr[k], xz_bytes(k))
        for dx in range(1, X):
            xo = lax.rem(xi + dx, X)
            if k in (0, 2):
                n = RS // 2
                for ct in range(2):
                    piece = span(dest[k], mult(RS * (2 * xo + ct) + q * n, n), n)
                    rcopy(piece, piece, gzs[k], gzr[k], rep=zp)
            else:
                _, w = rows_of(k)
                piece = span(dest[k], mult(w * xo + q * (w // 2), w // 2), w // 2)
                rcopy(piece, piece, gzs[k], gzr[k], rep=zp)
        if k > 1:
            finals.append(lambda: wait(gzs[k], xz_bytes(k)))

    def gather_core(k):
        if k in (0, 2):
            rows = mult(RS * f, RS)
            for src, sc, dc, w in cols(k, 1 - c):
                rcopy(
                    part(src, 0, RS, sc, w), part(dest[k], rows, RS, dc, w), gcs[k], gcr[k], fsdp=fs
                )
            for src, sc, dc, w in cols(k, c):
                lcopy(part(src, 0, RS, sc, w), part(dest[k], rows, RS, dc, w), gl[k])
            finals.append(lambda: wait(gcs[k], core_bytes(k)))
        else:
            src, w = rows_of(k)
            lcopy(span(src, mult(w * y, w), w), span(dest[k], mult(w * xi, w), w), gl[k])

    def gather_wait(k):
        wait(gl[k], local_bytes(k))
        if k in (0, 2):
            wait(gcr[k], core_bytes(k))
        wait(gzr[k], xz_bytes(k))

    xs = [S() for _ in range(NP)]
    xr = [S() for _ in range(NP)]
    zis = [S() for _ in range(NP)]
    zir = [S() for _ in range(NP)]
    zbs = [S() for _ in range(NP)]
    zbr = [S() for _ in range(NP)]
    ags = [S() for _ in range(NP)]
    agr = [S() for _ in range(NP)]
    agl = [S() for _ in range(NP)]
    lp = [S() for _ in range(2)]
    held = []

    h = NREP // 2
    depth = jnp.where(r < h, r, NREP - 1 - r)
    inner = jnp.where(r < h, r + 1, r - 1)
    outer = jnp.where(r < h, r - 1, r + 1)

    def is_up(p):
        return p < NU or p > 2 * NU

    def x_bytes():
        return gbuf.at[0, pl.ds(0, X - 1)]

    def send_x(p):
        for dx in range(1, X):
            xo = lax.rem(xi + dx, X)
            rcopy(gbuf.at[p, xo], xrecv.at[p, dx - 1], xs[p], xr[p], fsdp=2 * xo + c)
        finals.append(lambda: wait(xs[p], x_bytes()))

    def add_rows(count, fn):
        def step(i, carry):
            fn(ds(i, 64))
            return carry

        lax.fori_loop(0, count // 64, step, 0)

    def add_into(p, dst, other):
        def add(rows):
            dst[p, rows, :] = (own[p, rows, :].astype(F32) + other[p, rows, :].astype(F32)).astype(
                BF
            )

        add_rows(RX, add)

    def send_in(p, at_middle):
        if at_middle:
            rcopy(own.at[p], zback.at[p], zis[p], zbr[p], rep=inner)
        else:
            rcopy(own.at[p], zin.at[p], zis[p], zir[p], rep=inner)

    def stage_x(p):
        wait(xr[p], x_bytes())

        def add(rows):
            total = own[p, rows, :].astype(F32)
            for d in range(X - 1):
                total = total + xrecv[p, d, rows, :].astype(F32)
            own[p, rows, :] = total.astype(BF)

        add_rows(RX, add)

        @pl.when(depth == 0)
        def _():
            send_in(p, h == 1)

        finals.append(lambda: wait(zis[p], own.at[0]))

    def stage_in(k, p):
        @pl.when(depth == k)
        def _():
            wait(zir[p], own.at[0])
            add_into(p, own, zin)
            send_in(p, k == h - 1)

    def stage_out(i, p):
        @pl.when(depth == h - 1 - i)
        def _():
            wait(zbr[p], own.at[0])
            if i == 0:
                add_into(p, zback, zback)
            if h - 1 - i > 0:
                rcopy(zback.at[p], zback.at[p], zbs[p], zbr[p], rep=outer)

    def ag_bytes(p):
        return own.at[pl.ds(0, 3), pl.ds(0, RS)] if is_up(p) else own.at[0]

    def up_places(p):
        if p < NU:
            xx, off = p * PW // FX, p * PW % FX
            at = (FF // X) * xx + (FF // (2 * X)) * c + FX * y + off
            return [(0, PW, fin_up, mult(at, 128))]
        m = p - 2 * NU - 1
        if HX >= 128:
            return [
                (xx * HX, HX, fin_qkv, mult(D * m + (D // X) * xx + (D // (2 * X)) * c + HX * y, 128))
                for xx in range(X)
            ]
        return [(0, HC, fin_qkv, mult((2 * c + y) * 3 * HC + m * HC, 128))]

    def stage_ag(p):
        if is_up(p):
            for lane, w, dst, at in up_places(p):
                mine = zback.at[p, ds(c, RS), pl.ds(lane, w)]
                theirs = zback.at[p, ds(1 - c, RS), pl.ds(lane, w)]
                to = dst.at[:, pl.ds(at, w)]
                rcopy(mine, to, ags[p], agr[p], ctx=yo)
                rcopy(theirs, to, ags[p], agr[p], fsdp=fs, ctx=yo)
                rcopy(theirs, to, ags[p], agr[p], fsdp=fs)
                lcopy(mine, to, agl[p])
        else:
            if p < 2 * NU:
                pairs = [(zback.at[p], fin_dn.at[ds(y, RX), pl.ds((p - NU) * PW, PW)])]
            else:
                pairs = [
                    (
                        zback.at[p, pl.ds(b * HX, HX)],
                        fin_o.at[pl.ds(mult(y * HX, HX), HX), pl.ds(b * PW, PW)],
                    )
                    for b in range(RX // HX)
                ]
            for src, to in pairs:
                rcopy(src, to, ags[p], agr[p], ctx=yo)
                lcopy(src, to, agl[p])
        finals.append(lambda: wait(agl[p], own.at[0, pl.ds(0, RS)] if is_up(p) else own.at[0]))
        finals.append(lambda: wait(ags[p], ag_bytes(p)))
        finals.append(lambda: wait(agr[p], ag_bytes(p)))

    stages = [stage_x]
    for k in range(1, h):
        stages.append(functools.partial(stage_in, k))
    for i in range(h - 1):
        stages.append(functools.partial(stage_out, i))

    def stage_last(p):
        stage_out(h - 1, p)
        stage_ag(p)

    stages.append(stage_last)
    lag = [1] * len(stages)
    live = []
    moving = []
    ready = []
    clock = [0]

    def push():
        while ready and len(moving) < FLIGHT:
            send_x(ready[0])
            moving.append(ready.pop(0))

    def tick(count=1, drain=False):
        clock[0] += 1
        fresh = []
        for item in list(live):
            p, s, due = item
            if drain or clock[0] >= due:
                stages[s](p)
                if s == len(stages) - 1:
                    live.remove(item)
                else:
                    item[1:] = [s + 1, clock[0] + lag[s]]
        for _ in range(count):
            if moving:
                p = moving.pop(0)
                stages[0](p)
                push()
                fresh.append([p, 1, clock[0] + lag[0]])
        live.extend(fresh)

    def flush():
        while held:
            p, gst = held.pop(0)
            wait(lp[p % 2], gst)
            ready.append(p)
        push()

    def grad_piece(p, lhs_t, rhs, both):
        gst = both.at[p % 2]
        if is_up(p) or p < 2 * NU:

            def step(t, carry):
                gst[t] = mm(lhs_t[ds(t, RX), :], rhs()).astype(BF)
                return carry

            lax.fori_loop(0, X, step, 0)
        else:
            res = mm(lhs_t[...], rhs()).astype(BF)
            for xx in range(X):
                for b in range(RX // HX):
                    gst[xx, b * HX : (b + 1) * HX, :] = res[
                        xx * HX : (xx + 1) * HX, b * PW : (b + 1) * PW
                    ]
        own[p] = gst[xi]
        flush()
        lcopy(gst, gbuf.at[p], lp[p % 2])
        held.append((p, gst))

    bar = pltpu.get_barrier_semaphore()
    near = []
    for df in range(2 * X):
        for dy in range(2):
            if df or dy:
                near.append(dict(fsdp=lax.rem(f + df, 2 * X), ctx=lax.rem(y + dy, 2)))
    for dr in range(1, NREP):
        near.append(dict(rep=lax.rem(r + dr, NREP)))
    for dev in near:
        pl.semaphore_signal(bar, inc=1, device_id=dev, device_id_type=LINK)
    pl.semaphore_wait(bar, len(near))

    gather_x(0)
    tok = []
    home = ds(2 * c + y, R)
    for src, dst in ((x_ref, X4), (g_ref, G4)):
        ids = [S() for _ in range(7)]
        lcopy(src, dst.at[home], ids[0])
        rcopy(src, dst.at[home], ids[1], ids[2], fsdp=fs)
        rcopy(src, dst.at[home], ids[3], ids[4], ctx=yo)
        tok.append((src, dst, ids))
    s_sm, r_sm, l_sm = S(), S(), S()
    lcopy(sm_ref, sm_v.at[f], l_sm)
    for df in range(1, 2 * X):
        rcopy(sm_ref, sm_v.at[f], s_sm, r_sm, fsdp=lax.rem(f + df, 2 * X))
    s_oh, r_oh, l_oh = S(), S(), S()
    lcopy(oh_ref, oh_v.at[c], l_oh)
    rcopy(oh_ref, oh_v.at[c], s_oh, r_oh, fsdp=fs)
    for k in range(NG):
        gather_core(k)

    def exchange_forward():
        for src, dst, ids in tok:
            piece = dst.at[ds(2 * c + yo, R)]
            wait(ids[4], src)
            rcopy(piece, piece, ids[5], ids[6], fsdp=fs)

    def exchange_finish():
        for src, dst, ids in tok:
            wait(ids[6], src)

    wait(l_sm, sm_ref)
    wait(r_sm, sm_v.at[pl.ds(0, 2 * X - 1)])
    for ff in range(2 * X):
        vecs[:, ff * RS : (ff + 1) * RS] = sm_v[ff]
    sgv[...] = jnp.zeros_like(sgv)
    for src, dst, ids in tok:
        wait(ids[0], src)
        wait(ids[2], src)

    def vec(row):
        return vecs[row : row + 1, :]

    def center(blk):
        v = blk.astype(F32)
        mid = v - jnp.mean(v, -1, keepdims=True)
        rs = lax.rsqrt(jnp.mean(mid * mid, -1, keepdims=True) + EPSILON)
        return mid * rs, rs

    def norm_back(e, n, rs, gain, row):
        sgv[row : row + 1, :] += jnp.sum(e * n, 0, keepdims=True)
        sgv[row + 1 : row + 2, :] += jnp.sum(e, 0, keepdims=True)
        eg = e * gain
        return rs * (
            eg - jnp.mean(eg, -1, keepdims=True) - n * jnp.mean(eg * n, -1, keepdims=True)
        )

    def feed(n2t, hidt, gup, gst):
        def gsum(b, carry):
            at = pl.ds(mult((2 * c + y) * R + b * TT, TT), TT)
            sgv[4:5, :] += jnp.sum(G4[at, :].astype(F32), 0, keepdims=True)
            return carry

        lax.fori_loop(0, R // TT, gsum, 0)
        bias = jnp.concatenate(
            [
                jnp.where(
                    y == 0,
                    vecs[8 + rr : 9 + rr, ds(2 * xx + c, RS)],
                    vecs[10 + rr : 11 + rr, ds(2 * xx + c, RS)],
                )
                for xx in range(X)
                for rr in range(2)
            ],
            1,
        )
        gather_fwd(0)
        gather_x(1)
        gather_fwd(1)
        gather_x(2)
        gather_x(3)
        gather_wait(0)
        gather_wait(1)
        half_tiles = T // TT // 2

        def tile(i, gb):
            @pl.when(i == half_tiles - 1)
            def _():
                exchange_forward()

            @pl.when(i == half_tiles)
            def _():
                exchange_finish()

            yy = jnp.where(i < half_tiles, y, yo)
            j = lax.rem(i, half_tiles)
            per = R // TT
            rows = pl.ds(mult((2 * lax.div(j, per) + yy) * R + lax.rem(j, per) * TT, TT), TT)
            n, rs = center(X4[rows, :])
            n2 = (n * vec(2) + vec(3)).astype(BF)
            n2t[:, rows] = n2.T
            up = mm(n2, wup[...]) + bias
            cdf = 0.5 + 0.5 * lax.erf(up * (1.0 / math.sqrt(2.0)))
            hd = (up * cdf).astype(BF)
            hidt[:, rows] = hd.T
            gh = mm(G4[rows, :], wdn[...], NT)
            pdf = jnp.exp(-0.5 * up * up) * (1.0 / math.sqrt(2.0 * math.pi))
            gu = (gh * (cdf + up * pdf)).astype(BF)
            gup[rows, :] = gu
            OB[rows, :] = mm(hd, wdn[...]).astype(BF)
            gn = mm(gu, wup[...], NT)
            TB[rows, :] = norm_back(gn, n, rs, vec(2), 2).astype(BF)
            return gb + jnp.sum(gu.astype(F32), 0, keepdims=True)

        gb = lax.fori_loop(0, T // TT, tile, jnp.zeros((1, FL), F32))
        for yy in range(2):

            @pl.when(y == yy)
            def _():
                for xx in range(X):
                    for rr in range(2):
                        at = (2 * xx + rr) * RS
                        row = 5 + 2 * yy + rr
                        sgv[row : row + 1, ds(2 * xx + c, RS)] = gb[:, at : at + RS]

        gather_fwd(2)
        gather_fwd(3)
        for t in range(NU):
            grad_piece(t, n2t, lambda: gup[:, t * PW : (t + 1) * PW], gst)
        for t in range(NU):
            tick(1)
            grad_piece(NU + t, hidt, lambda: G4[:, t * PW : (t + 1) * PW], gst)
        flush()

    pl.run_scoped(
        feed,
        pltpu.VMEM((D, T), BF),
        pltpu.VMEM((FL, T), BF),
        pltpu.VMEM((T, FL), BF),
        pltpu.VMEM((2, X, RX, PW), BF),
    )

    s_mo = [S() for _ in range(2)]
    r_mo = [S() for _ in range(2)]
    s_af = [S() for _ in range(2)]
    r_af = [S() for _ in range(2)]
    l_tab, l_st, l_fin = S(), S(), S()
    s_sga, r_sga, l_sga = S(), S(), S()
    s_sgb, r_sgb, l_sgb = S(), S(), S()

    def give(a, buf):
        rcopy(buf.at[ds(1 - c, L)], mo.at[a], s_mo[a], r_mo[a], fsdp=fs)

    def take(a, buf, room):
        wait(r_mo[a], mo.at[a])
        wait(gzs[a], xz_bytes(a))
        lcopy(mo.at[a], room.at[pl.ds(0, L)], l_st).wait()

        def add(i, carry):
            rows = pl.ds(mult(c * L + i * 64, 64), 64)
            buf[rows, :] = (buf[rows, :].astype(F32) + room[ds(i, 64), :].astype(F32)).astype(BF)
            return carry

        lax.fori_loop(0, L // 64, add, 0)
        rcopy(buf.at[ds(2 * c + yo, R)], af.at[a], s_af[a], r_af[a], ctx=yo)

    def last(a, buf, room, dst):
        wait(r_af[a], af.at[a])
        lcopy(af.at[a], room.at[pl.ds(0, R)], l_st).wait()

        def add(i, carry):
            rows = pl.ds(mult((2 * c + y) * R + i * 64, 64), 64)
            total = buf[rows, :].astype(F32) + room[ds(i, 64), :].astype(F32)
            if a == 0:
                total = total + X4[rows, :].astype(F32) + vec(7) + vec(12)
            else:
                total = total + G4[rows, :].astype(F32)
            room[ds(i, 64), :] = total.astype(BF)
            return carry

        lax.fori_loop(0, R // 64, add, 0)
        lcopy(room.at[pl.ds(0, R)], dst, l_fin)

    def attend(n1t, ga, qkv, ctx, ctxt, gctx, gproj, dkv, tab, gst):
        lcopy(tab_ref, tab, l_tab)
        wait(l_oh, oh_ref)
        wait(r_oh, oh_ref)

        def weight(cc, b, s, width):
            w = oh_v[cc, pl.ds(b * NB + s, 1), :].astype(BF)
            return jnp.concatenate([w] * (width // 128), 1)

        def in_order(ref, cc, b):
            total = None
            for s in range(NB):
                rows = pl.ds(mult(cc * L + s * TT, TT), TT)
                term = ref[rows, :] * weight(cc, b, s, D)
                total = term if total is None else total + term
            return total

        def in_slot(ref, cc, s, width):
            total = None
            for b in range(NB):
                rows = pl.ds(mult(cc * L + b * TT, TT), TT)
                term = ref[rows, :] * weight(cc, b, s, width)
                total = term if total is None else total + term
            return total

        def turned(v, rows, sign):
            right = pltpu.roll(v, ROT // 2, 1)
            left = pltpu.roll(v, 128 - ROT // 2, 1)
            return v * tab[0, rows, :] + sign * (
                right * tab[1, rows, :] + left * tab[2, rows, :]
            )

        def pick(options):
            a = jnp.where(c == 0, options[0], options[2])
            b = jnp.where(c == 0, options[1], options[3])
            return jnp.where(y == 0, a, b)

        def spot(m, xx, cc, yy):
            e = D * m + (D // X) * xx + (D // (2 * X)) * cc + HX * yy
            rest = e % (3 * RS)
            return e // (3 * RS), rest // RS, rest % RS

        bias = jnp.concatenate(
            [
                pick(
                    [
                        jnp.concatenate(
                            [
                                sm_v[ff, 4 + row : 5 + row, lane : lane + HX]
                                for ff, row, lane in [spot(m, xx, cc, yy) for xx in range(X)]
                            ],
                            1,
                        )
                        for cc in range(2)
                        for yy in range(2)
                    ]
                )
                for m in range(3)
            ],
            1,
        )
        wait(l_tab, tab_ref)
        gather_wait(2)
        gather_wait(3)

        def prep(t, carry):
            cc, b = lax.div(t, NB), lax.rem(t, NB)
            n, _ = center(in_order(X4, cc, b))
            n1 = (n * vec(0) + vec(1)).astype(BF)
            n1t[:, ds(t)] = n1.T
            gv = in_order(G4, cc, b)
            ga[ds(t), :] = gv
            v = mm(n1, wqkv[...]) + bias
            for m in range(2):
                for u in range(HC // 128):
                    w = turned(v[:, m * HC + u * 128 : m * HC + (u + 1) * 128], ds(b), 1.0)
                    if m == 0:
                        w = w * (1.0 / math.sqrt(HEAD))
                    qkv[m, ds(t), u * 128 : (u + 1) * 128] = w.astype(BF)
            qkv[2, ds(t), :] = v[:, 2 * HC :].astype(BF)
            gctx[ds(t), :] = mm(gv, wo[...], NT).astype(BF)
            return carry

        lax.fori_loop(0, T // TT, prep, 0)
        tick(1)

        low_half = lax.broadcasted_iota(jnp.int32, (1, 128), 1) < HEAD
        dkv[...] = jnp.zeros_like(dkv)
        pairs = HC // 128
        for i in range(NB):
            n = (i + 1) * TT

            def pair(u, carry):
                cc, hp = lax.div(u, pairs), lax.rem(u, pairs)
                lanes = pl.ds(mult(hp * 128, 128), 128)
                rows = pl.ds(mult(cc * L + i * TT, TT), TT)
                seen = pl.ds(mult(cc * L, L), n)
                qb = qkv[0, rows, lanes]
                gb = gctx[rows, lanes]
                kb = qkv[1, seen, lanes]
                vb = qkv[2, seen, lanes]
                ahead = lax.broadcasted_iota(jnp.int32, (TT, n), 1) - lax.broadcasted_iota(
                    jnp.int32, (TT, n), 0
                )
                zero = jnp.zeros_like(qb)
                res = []
                for hd in range(2):
                    mask = low_half if hd == 0 else jnp.logical_not(low_half)
                    s = mm(jnp.where(mask, qb, zero), kb, NT)
                    s = jnp.where(ahead <= i * TT, s, -1e30)
                    p = jnp.exp(s - jnp.max(s, -1, keepdims=True))
                    p = p * (1.0 / jnp.sum(p, -1, keepdims=True))
                    pb = p.astype(BF)
                    dp = mm(jnp.where(mask, gb, zero), vb, NT)
                    dsc = (p * (dp - jnp.sum(p * dp, -1, keepdims=True))).astype(BF)
                    res.append((mm(pb, vb), mm(dsc, kb), mm(dsc, qb, TN), mm(pb, gb, TN)))
                both = [jnp.where(low_half, u0, u1) for u0, u1 in zip(res[0], res[1])]
                cb = both[0].astype(BF)
                ctx[rows, lanes] = cb
                ctxt[lanes, rows] = cb.T
                dq = turned(both[1] * (1.0 / math.sqrt(HEAD)), pl.ds(i * TT, TT), -1.0)
                gproj[rows, lanes] = dq.astype(BF)
                dkv[0, seen, lanes] += both[2]
                dkv[1, seen, lanes] += both[3]
                return carry

            lax.fori_loop(0, 2 * pairs, pair, 0)
            tick(1)

        def turn_back(t, carry):
            b = lax.rem(t, NB)
            for u in range(pairs):
                at = pl.ds(u * 128, 128)
                gproj[ds(t), HC + u * 128 : HC + (u + 1) * 128] = turned(
                    dkv[0, ds(t), at], ds(b), -1.0
                ).astype(BF)
            gproj[ds(t), 2 * HC : 3 * HC] = dkv[1, ds(t), :].astype(BF)
            return carry

        lax.fori_loop(0, T // TT, turn_back, 0)

        grad_piece(2 * NU, ctxt, lambda: ga[...], gst)
        for m in range(3):
            grad_piece(2 * NU + 1 + m, n1t, lambda: gproj[:, m * HC : (m + 1) * HC], gst)
        flush()

        def att_out(t, carry):
            cc, s = lax.div(t, NB), lax.rem(t, NB)
            a = mm(in_slot(ctx, cc, s, HC), wo[...])
            OB[ds(t), :] = (OB[ds(t), :].astype(F32) + a).astype(BF)
            return carry

        lax.fori_loop(0, T // TT, att_out, 0)
        give(0, OB)
        tick(1)

        def att_in(t, carry):
            cc, s = lax.div(t, NB), lax.rem(t, NB)
            e = mm(in_slot(gproj, cc, s, 3 * HC), wqkv[...], NT)
            n, rs = center(X4[ds(t), :])
            term = norm_back(e, n, rs, vec(0), 0)
            TB[ds(t), :] = (TB[ds(t), :].astype(F32) + term).astype(BF)
            return carry

        take(0, OB, wup)
        lax.fori_loop(0, T // TT, att_in, 0)
        give(1, TB)

        for m in range(3):
            gb = jnp.sum(gproj[:, m * HC : (m + 1) * HC].astype(F32), 0, keepdims=True)
            for cc in range(2):
                for yy in range(2):

                    @pl.when((c == cc) & (y == yy))
                    def _():
                        for xx in range(X):
                            ff, row, lane = spot(m, xx, cc, yy)
                            at = ff * RS + lane
                            sgv[9 + row : 10 + row, at : at + HX] = gb[:, xx * HX : (xx + 1) * HX]

    pl.run_scoped(
        attend,
        pltpu.VMEM((D, T), BF),
        pltpu.VMEM((T, D), BF),
        pltpu.VMEM((3, T, HC), BF),
        pltpu.VMEM((T, HC), BF),
        pltpu.VMEM((HC, T), BF),
        pltpu.VMEM((T, HC), BF),
        pltpu.VMEM((T, 3 * HC), BF),
        pltpu.VMEM((2, T, HC), F32),
        pltpu.VMEM((3, L, 128), F32),
        pltpu.VMEM((2, X, RX, PW), BF),
    )

    here = f * 2 + y
    lcopy(sgv, sgA.at[here], l_sga)
    for dev in near[: 4 * X - 1]:
        rcopy(sgv, sgA.at[here], s_sga, r_sga, **dev)
    tick(1)
    take(1, TB, wdn)
    wait(l_sga, sgv)
    wait(r_sga, sgA.at[pl.ds(0, 4 * X - 1)])
    total = sgA[0]
    for i in range(1, 4 * X):
        total = total + sgA[i]
    wait(s_sga, sgA.at[pl.ds(0, 4 * X - 1)])
    sgv[...] = total
    lcopy(sgv, sgB.at[r], l_sgb)
    for dev in near[4 * X - 1 :]:
        rcopy(sgv, sgB.at[r], s_sgb, r_sgb, **dev)
    tick(1)
    tick(1, True)
    tick(1, True)
    last(0, OB, wup, out_ref)
    wait(l_sgb, sgv)
    wait(r_sgb, sgB.at[pl.ds(0, NREP - 1)])
    wait(s_sgb, sgB.at[pl.ds(0, NREP - 1)])
    total = sgB[0]
    for i in range(1, NREP):
        total = total + sgB[i]
    sgv[...] = total
    lcopy(sgv, sg_ref, l_sga)
    while live or moving or ready:
        tick(1, True)
    last(1, TB, wdn, gin_ref)

    wait(l_sga, sgv)
    wait(l_fin, af)
    for a in range(2):
        wait(s_mo[a], mo.at[a])
        wait(s_af[a], af.at[a])
    wait(s_sm, sm_v.at[pl.ds(0, 2 * X - 1)])
    wait(s_oh, oh_ref)
    for src, dst, ids in tok:
        for k in (1, 3, 5):
            wait(ids[k], src)
    for fn in finals:
        fn()

    @pl.when(depth > 0)
    def _():
        for p in range(NP):
            wait(zbs[p], own.at[0])


def sem_count(NP):
    return 7 * 4 + 9 * NP + 64


def body(
    residual_in,
    block_order,
    ln1_gain,
    ln1_bias,
    ln2_gain,
    ln2_bias,
    w_qkv,
    b_qkv,
    w_out,
    b_out,
    w_up,
    b_up,
    w_down,
    b_down,
    cotangent,
):
    R, D = residual_in.shape[1:]
    FF = w_up.shape[1]
    NF = lax.axis_size("fsdp")
    NREP = lax.axis_size("rep")
    X = NF // 2
    L, T, RX, RS = 2 * R, 4 * R, D // X, D // NF
    FL, HC = FF // 4, D // 4
    HX = HC // X
    NP = 2 * (FL // PW) + 4
    f = lax.axis_index("fsdp")

    order = block_order[0]
    count = order.shape[0]
    spots = jnp.arange(count, dtype=jnp.int32)
    where = (order[None, :] == spots[:, None]).astype(F32).reshape(-1, 1)
    where = jnp.broadcast_to(where, (count * count, 128))
    small, at = None, 0
    for v in (ln1_gain, ln1_bias, ln2_gain, ln2_bias, b_qkv, b_out, b_up, b_down):
        n = v.shape[0]
        term = jnp.pad(v.astype(F32), (at, 16 * RS - at - n))
        small = term if small is None else small + term
        at += n
    small = small.reshape(16, RS)
    halves = ROT // 2
    lane = np.arange(128) % HEAD
    angles = np.arange(L)[:, None] * 10000.0 ** (-2.0 * (lane % halves) / ROT)[None, :]
    cosine, sine = np.cos(angles), np.sin(angles)
    tab = np.stack(
        [
            np.where(lane < ROT, cosine, 1.0),
            np.where((lane < ROT) & (lane >= halves), sine, 0.0),
            np.where(lane < halves, -sine, 0.0),
        ]
    ).astype(np.float32)

    def columns(w):
        if HX >= 128:
            return w
        w = w.reshape(RS, 3, X, 2, 2, HX).transpose(0, 3, 4, 1, 2, 5)
        return w.reshape(RS, 3 * D)

    def columns_back(w):
        if HX >= 128:
            return w
        w = w.reshape(RS, 2, 2, 3, X, HX).transpose(0, 3, 4, 1, 2, 5)
        return w.reshape(RS, 3 * D)

    anywhere = pl.BlockSpec(memory_space=pl.ANY)
    sds = jax.ShapeDtypeStruct
    outs = pl.pallas_call(
        functools.partial(kernel, (X, NREP, R, D, FF)),
        out_shape=(
            sds((RS, FF), BF),
            sds((FF // NF, D), BF),
            sds((RS, 3 * D), BF),
            sds((RS, D), BF),
            sds((R, D), BF),
            sds((R, D), BF),
            sds((16, D), F32),
            sds((NP, X, RX, PW), BF),
            sds((2, L, D), BF),
            sds((2, R, D), BF),
        ),
        in_specs=[anywhere] * 9,
        out_specs=(anywhere,) * 10,
        scratch_shapes=[
            pltpu.VMEM((T, D), BF),
            pltpu.VMEM((T, D), BF),
            pltpu.VMEM((D, FL), BF),
            pltpu.VMEM((FL, D), BF),
            pltpu.VMEM((D, 3 * HC), BF),
            pltpu.VMEM((HC, D), BF),
            pltpu.VMEM((2, (L // TT) ** 2, 128), F32),
            pltpu.VMEM((NF, 16, RS), F32),
            pltpu.VMEM((16, D), F32),
            pltpu.VMEM((16, D), F32),
            pltpu.VMEM((2 * NF, 16, D), F32),
            pltpu.VMEM((NREP, 16, D), F32),
            pltpu.VMEM((NP, RX, PW), BF),
            pltpu.VMEM((NP, RX, PW), BF),
            pltpu.VMEM((NP, RX, PW), BF),
            pltpu.VMEM((NP, X - 1, RX, PW), BF),
            pltpu.VMEM((T, D), BF),
            pltpu.VMEM((T, D), BF),
            pltpu.SemaphoreType.DMA((sem_count(NP),)),
        ],
        compiler_params=pltpu.CompilerParams(
            collective_id=0, has_side_effects=True, vmem_limit_bytes=63 * 1024 * 1024
        ),
    )(
        residual_in.reshape(R, D),
        cotangent.reshape(R, D),
        where,
        small,
        columns(w_qkv),
        w_out,
        w_up,
        w_down,
        tab,
    )
    fin_up, fin_dn, fin_qkv, fin_o, out, gin, sg = outs[:7]
    mine = lax.dynamic_slice(sg, (0, f * RS), (16, RS))
    return (
        out[None],
        gin.astype(F32)[None],
        mine[0],
        mine[1],
        mine[2],
        mine[3],
        columns_back(fin_qkv).astype(F32),
        mine[9:12].reshape(-1),
        fin_o.astype(F32),
        mine[4],
        fin_up.astype(F32),
        mine[5:9].reshape(-1),
        fin_dn.astype(F32),
        mine[4],
    )


def solution(mesh):
    in_specs = (
        P(("rep", "fsdp"), "ctx", None),
        P(("rep", "fsdp"), None),
        P("fsdp"),
        P("fsdp"),
        P("fsdp"),
        P("fsdp"),
        P("fsdp", None),
        P("fsdp"),
        P("fsdp", None),
        P("fsdp"),
        P("fsdp", None),
        P("fsdp"),
        P("fsdp", None),
        P("fsdp"),
        P(("rep", "fsdp"), "ctx", None),
    )
    out_specs = (
        P(("rep", "fsdp"), "ctx", None),
        P(("rep", "fsdp"), "ctx", None),
        P("fsdp"),
        P("fsdp"),
        P("fsdp"),
        P("fsdp"),
        P("fsdp", None),
        P("fsdp"),
        P("fsdp", None),
        P("fsdp"),
        P("fsdp", None),
        P("fsdp"),
        P("fsdp", None),
        P("fsdp"),
    )
    return jax.shard_map(body, mesh=mesh, in_specs=in_specs, out_specs=out_specs, check_vma=False)
```

```python
import functools
import math

import jax
import jax.numpy as jnp
import numpy as np
from jax import lax
from jax.experimental import pallas as pl
from jax.experimental.pallas import tpu as pltpu
from jax.sharding import PartitionSpec as P

HEADS = 16
HEAD = 64
ROT = 16
BLK = 256
EPSILON = 1e-05
PW = 256
TT = 256
FLIGHT = 4
LINK = pl.DeviceIdType.MESH
BF = jnp.bfloat16
F32 = jnp.float32

NN = (((1,), (0,)), ((), ()))
NT = (((1,), (1,)), ((), ()))
TN = (((0,), (0,)), ((), ()))


def mm(a, b, dims=NN):
    return lax.dot_general(a, b, dims, preferred_element_type=F32)


def mult(value, of):
    return value if isinstance(value, int) else pl.multiple_of(value, of)


def kernel(
    dims,
    x_ref,
    g_ref,
    oh_ref,
    sm_ref,
    wqkv_ref,
    wo_ref,
    wup_ref,
    wdn_ref,
    tab_ref,
    fin_up,
    fin_dn,
    fin_qkv,
    fin_o,
    out_ref,
    gin_ref,
    sg_ref,
    gbuf,
    mo,
    af,
    X4,
    G4,
    wup,
    wdn,
    wqkv,
    wo,
    oh_v,
    sm_v,
    vecs,
    sgv,
    sgA,
    sgB,
    own,
    zin,
    zback,
    xrecv,
    OB,
    TB,
    sems,
):
    X, NREP, R, D, FF = dims
    L = 2 * R
    T = 2 * L
    RX = D // X
    RS = D // (2 * X)
    FL = FF // 4
    HC = D // 4
    FX, HX = FL // X, HC // X
    NB = L // TT
    NU = FL // PW
    NP = 2 * NU + 4

    f = lax.axis_index("fsdp")
    y = lax.axis_index("ctx")
    r = lax.axis_index("rep")
    c = lax.rem(f, 2)
    xi = lax.div(f, 2)
    fs = xi * 2 + (1 - c)
    yo = 1 - y

    counter = [0]

    def S():
        counter[0] += 1
        return counter[0] - 1

    def rcopy(src, dst, ss, rs, **dev):
        cp = pltpu.make_async_remote_copy(
            src_ref=src,
            dst_ref=dst,
            send_sem=sems.at[ss],
            recv_sem=sems.at[rs],
            device_id=dev,
            device_id_type=LINK,
        )
        cp.start()
        return cp

    def lcopy(src, dst, s):
        cp = pltpu.make_async_copy(src, dst, sems.at[s])
        cp.start()
        return cp

    def wait(s, ref):
        pltpu.make_async_copy(ref, ref, sems.at[s]).wait()

    def ds(i, size=TT):
        return pl.ds(mult(i * size, size), size)

    finals = []

    NG = 4
    units = [(0, 0), (0, 1), (1, 0), (1, 1), (2, 0), (3, 0)]
    cuts = [2, 2, 1, 1]
    gxs = [S() for _ in units]
    gxr = [S() for _ in units]
    gzs = [S() for _ in units]
    gzr = [S() for _ in units]
    gcs = [S() for _ in range(NG)]
    gcr = [S() for _ in range(NG)]
    gl = [S() for _ in range(NG)]
    q = lax.rem(r, 2)
    zp = r + 1 - 2 * q
    dest = [wup, wdn, wqkv, wo]

    def cols(k, ct):
        if k == 0:
            for xx in range(X):
                at = (FF // X) * xx + (FF // (2 * X)) * ct + FX * y
                yield wup_ref, mult(at, 128), xx * FX, FX
        elif HX >= 128:
            for m in range(3):
                for xx in range(X):
                    at = D * m + (D // X) * xx + (D // (2 * X)) * ct + HX * y
                    yield wqkv_ref, mult(at, 128), m * HC + xx * HX, HX
        else:
            yield wqkv_ref, mult((2 * ct + y) * 3 * HC, 128), 0, 3 * HC

    def part(ref, row, n, col, w):
        return ref.at[pl.ds(row, n), pl.ds(col, w)]

    def span(ref, row, n):
        return ref.at[pl.ds(row, n)]

    def xz_bytes(k):
        if k < 2:
            return gbuf.at[0, pl.ds(0, X - 1)]
        return gbuf.at[pl.ds(0, 3 if k == 2 else 1), pl.ds(0, X - 1), pl.ds(0, RX // 2)]

    def core_bytes(k):
        if k == 0:
            return gbuf.at[pl.ds(0, 2), 0]
        return gbuf.at[pl.ds(0, 3), 0, pl.ds(0, RX // 2)]

    def local_bytes(k):
        if k == 2:
            return core_bytes(k)
        return gbuf.at[pl.ds(0, (2, 4, 0, 1)[k]), 0]

    def rows_of(k):
        return (wdn_ref, FX) if k == 1 else (wo_ref, HX)

    def gather_x(u):
        k, cut = units[u]
        for dx in range(1, X):
            xo = lax.rem(xi + dx, X)
            if k in (0, 2):
                n = RS // 2 // cuts[k]
                r0 = mult(q * (RS // 2) + cut * n, n)
                for ct in range(2):
                    for src, sc, dc, w in cols(k, ct):
                        rcopy(
                            part(src, r0, n, sc, w),
                            part(dest[k], mult(RS * f + r0, n), n, dc, w),
                            gxs[u],
                            gxr[u],
                            fsdp=2 * xo + ct,
                        )
            else:
                src, w = rows_of(k)
                n = w // 2 // cuts[k]
                r0 = q * (w // 2) + cut * n
                rcopy(
                    span(src, mult(w * y + r0, n), n),
                    span(dest[k], mult(w * xi + r0, n), n),
                    gxs[u],
                    gxr[u],
                    fsdp=2 * xo + c,
                )
        finals.append(lambda: wait(gxs[u], xz_bytes(k)))

    def gather_fwd(u):
        k, cut = units[u]
        wait(gxr[u], xz_bytes(k))
        for dx in range(1, X):
            xo = lax.rem(xi + dx, X)
            if k in (0, 2):
                n = RS // 2 // cuts[k]
                r0 = q * (RS // 2) + cut * n
                for ct in range(2):
                    piece = span(dest[k], mult(RS * (2 * xo + ct) + r0, n), n)
                    rcopy(piece, piece, gzs[u], gzr[u], rep=zp)
            else:
                _, w = rows_of(k)
                n = w // 2 // cuts[k]
                piece = span(dest[k], mult(w * xo + q * (w // 2) + cut * n, n), n)
                rcopy(piece, piece, gzs[u], gzr[u], rep=zp)
        if k > 1:
            finals.append(lambda: wait(gzs[u], xz_bytes(k)))

    def gather_core(k):
        if k in (0, 2):
            rows = mult(RS * f, RS)
            for src, sc, dc, w in cols(k, 1 - c):
                rcopy(
                    part(src, 0, RS, sc, w), part(dest[k], rows, RS, dc, w), gcs[k], gcr[k], fsdp=fs
                )
            for src, sc, dc, w in cols(k, c):
                lcopy(part(src, 0, RS, sc, w), part(dest[k], rows, RS, dc, w), gl[k])
            finals.append(lambda: wait(gcs[k], core_bytes(k)))
        else:
            src, w = rows_of(k)
            lcopy(span(src, mult(w * y, w), w), span(dest[k], mult(w * xi, w), w), gl[k])

    def gather_wait(k):
        wait(gl[k], local_bytes(k))
        if k in (0, 2):
            wait(gcr[k], core_bytes(k))
        for u, (kk, _) in enumerate(units):
            if kk == k:
                wait(gzr[u], xz_bytes(k))

    xs = [S() for _ in range(NP)]
    xr = [S() for _ in range(NP)]
    zis = [S() for _ in range(NP)]
    zir = [S() for _ in range(NP)]
    zbs = [S() for _ in range(NP)]
    zbr = [S() for _ in range(NP)]
    ags = [S() for _ in range(NP)]
    agr = [S() for _ in range(NP)]
    agl = [S() for _ in range(NP)]
    lp = [S() for _ in range(2)]
    held = []
    made = [0]

    h = NREP // 2
    depth = jnp.where(r < h, r, NREP - 1 - r)
    inner = jnp.where(r < h, r + 1, r - 1)
    outer = jnp.where(r < h, r - 1, r + 1)

    def is_up(p):
        return p < NU or p > 2 * NU

    def x_bytes():
        return gbuf.at[0, pl.ds(0, X - 1)]

    def send_x(p):
        for dx in range(1, X):
            xo = lax.rem(xi + dx, X)
            rcopy(gbuf.at[p, xo], xrecv.at[p, dx - 1], xs[p], xr[p], fsdp=2 * xo + c)
        finals.append(lambda: wait(xs[p], x_bytes()))

    def add_rows(count, fn):
        def step(i, carry):
            fn(ds(i, 64))
            return carry

        lax.fori_loop(0, count // 64, step, 0)

    def add_into(p, dst, other):
        def add(rows):
            dst[p, rows, :] = (own[p, rows, :].astype(F32) + other[p, rows, :].astype(F32)).astype(
                BF
            )

        add_rows(RX, add)

    def send_in(p, at_middle):
        if at_middle:
            rcopy(own.at[p], zback.at[p], zis[p], zbr[p], rep=inner)
        else:
            rcopy(own.at[p], zin.at[p], zis[p], zir[p], rep=inner)

    def stage_x(p):
        wait(xr[p], x_bytes())

        def add(rows):
            total = own[p, rows, :].astype(F32)
            for d in range(X - 1):
                total = total + xrecv[p, d, rows, :].astype(F32)
            own[p, rows, :] = total.astype(BF)

        add_rows(RX, add)

        @pl.when(depth == 0)
        def _():
            send_in(p, h == 1)

        finals.append(lambda: wait(zis[p], own.at[0]))

    def stage_in(k, p):
        @pl.when(depth == k)
        def _():
            wait(zir[p], own.at[0])
            add_into(p, own, zin)
            send_in(p, k == h - 1)

    def stage_out(i, p):
        @pl.when(depth == h - 1 - i)
        def _():
            wait(zbr[p], own.at[0])
            if i == 0:
                add_into(p, zback, zback)
            if h - 1 - i > 0:
                rcopy(zback.at[p], zback.at[p], zbs[p], zbr[p], rep=outer)

    def ag_bytes(p):
        return own.at[pl.ds(0, 3), pl.ds(0, RS)] if is_up(p) else own.at[0]

    def up_places(p):
        if p < NU:
            xx, off = p * PW // FX, p * PW % FX
            at = (FF // X) * xx + (FF // (2 * X)) * c + FX * y + off
            return [(0, PW, fin_up, mult(at, 128))]
        m = p - 2 * NU - 1
        if HX >= 128:
            return [
                (xx * HX, HX, fin_qkv, mult(D * m + (D // X) * xx + (D // (2 * X)) * c + HX * y, 128))
                for xx in range(X)
            ]
        return [(0, HC, fin_qkv, mult((2 * c + y) * 3 * HC + m * HC, 128))]

    def stage_ag(p):
        if is_up(p):
            for lane, w, dst, at in up_places(p):
                mine = zback.at[p, ds(c, RS), pl.ds(lane, w)]
                theirs = zback.at[p, ds(1 - c, RS), pl.ds(lane, w)]
                to = dst.at[:, pl.ds(at, w)]
                rcopy(mine, to, ags[p], agr[p], ctx=yo)
                rcopy(theirs, to, ags[p], agr[p], fsdp=fs, ctx=yo)
                rcopy(theirs, to, ags[p], agr[p], fsdp=fs)
                lcopy(mine, to, agl[p])
        else:
            if p < 2 * NU:
                pairs = [(zback.at[p], fin_dn.at[ds(y, RX), pl.ds((p - NU) * PW, PW)])]
            else:
                pairs = [
                    (
                        zback.at[p, pl.ds(b * HX, HX)],
                        fin_o.at[pl.ds(mult(y * HX, HX), HX), pl.ds(b * PW, PW)],
                    )
                    for b in range(RX // HX)
                ]
            for src, to in pairs:
                rcopy(src, to, ags[p], agr[p], ctx=yo)
                lcopy(src, to, agl[p])
        finals.append(lambda: wait(agl[p], own.at[0, pl.ds(0, RS)] if is_up(p) else own.at[0]))
        finals.append(lambda: wait(ags[p], ag_bytes(p)))
        finals.append(lambda: wait(agr[p], ag_bytes(p)))

    stages = [stage_x]
    for k in range(1, h):
        stages.append(functools.partial(stage_in, k))
    for i in range(h - 1):
        stages.append(functools.partial(stage_out, i))

    def stage_last(p):
        stage_out(h - 1, p)
        stage_ag(p)

    stages.append(stage_last)
    lag = [1] * len(stages)
    live = []
    moving = []
    ready = []
    clock = [0]

    def push():
        while ready and len(moving) < FLIGHT:
            send_x(ready[0])
            moving.append(ready.pop(0))

    def tick(count=1, drain=False):
        clock[0] += 1
        fresh = []
        for item in list(live):
            p, s, due = item
            if drain or clock[0] >= due:
                stages[s](p)
                if s == len(stages) - 1:
                    live.remove(item)
                else:
                    item[1:] = [s + 1, clock[0] + lag[s]]
        for _ in range(count):
            if moving:
                p = moving.pop(0)
                stages[0](p)
                push()
                fresh.append([p, 1, clock[0] + lag[0]])
        live.extend(fresh)

    def flush():
        while held:
            p, b, gst = held.pop(0)
            wait(lp[b], gst)
            ready.append(p)
        push()

    def grad_piece(p, lhs_t, rhs, both):
        made[0] += 1
        turn = made[0] % 2
        gst = both.at[turn]
        if is_up(p) or p < 2 * NU:

            def step(t, carry):
                gst[t] = mm(lhs_t[ds(t, RX), :], rhs()).astype(BF)
                return carry

            lax.fori_loop(0, X, step, 0)
        else:
            res = mm(lhs_t[...], rhs()).astype(BF)
            for xx in range(X):
                for b in range(RX // HX):
                    gst[xx, b * HX : (b + 1) * HX, :] = res[
                        xx * HX : (xx + 1) * HX, b * PW : (b + 1) * PW
                    ]
        own[p] = gst[xi]
        flush()
        lcopy(gst, gbuf.at[p], lp[turn])
        held.append((p, turn, gst))

    bar = pltpu.get_barrier_semaphore()
    near = []
    for df in range(2 * X):
        for dy in range(2):
            if df or dy:
                near.append(dict(fsdp=lax.rem(f + df, 2 * X), ctx=lax.rem(y + dy, 2)))
    for dr in range(1, NREP):
        near.append(dict(rep=lax.rem(r + dr, NREP)))
    for dev in near:
        pl.semaphore_signal(bar, inc=1, device_id=dev, device_id_type=LINK)
    pl.semaphore_wait(bar, len(near))

    gather_x(0)
    gather_x(1)
    tok = []
    home = ds(2 * c + y, R)
    for src, dst in ((x_ref, X4), (g_ref, G4)):
        ids = [S() for _ in range(7)]
        lcopy(src, dst.at[home], ids[0])
        rcopy(src, dst.at[home], ids[1], ids[2], fsdp=fs)
        rcopy(src, dst.at[home], ids[3], ids[4], ctx=yo)
        tok.append((src, dst, ids))
    s_sm, r_sm, l_sm = S(), S(), S()
    lcopy(sm_ref, sm_v.at[f], l_sm)
    for df in range(1, 2 * X):
        rcopy(sm_ref, sm_v.at[f], s_sm, r_sm, fsdp=lax.rem(f + df, 2 * X))
    s_oh, r_oh, l_oh = S(), S(), S()
    lcopy(oh_ref, oh_v.at[c], l_oh)
    rcopy(oh_ref, oh_v.at[c], s_oh, r_oh, fsdp=fs)
    for k in range(NG):
        gather_core(k)

    def exchange_forward():
        for src, dst, ids in tok:
            piece = dst.at[ds(2 * c + yo, R)]
            wait(ids[4], src)
            rcopy(piece, piece, ids[5], ids[6], fsdp=fs)

    def exchange_finish():
        for src, dst, ids in tok:
            wait(ids[6], src)

    wait(l_sm, sm_ref)
    wait(r_sm, sm_v.at[pl.ds(0, 2 * X - 1)])
    for ff in range(2 * X):
        vecs[:, ff * RS : (ff + 1) * RS] = sm_v[ff]
    sgv[...] = jnp.zeros_like(sgv)
    for src, dst, ids in tok:
        wait(ids[0], src)
        wait(ids[2], src)

    def vec(row):
        return vecs[row : row + 1, :]

    def center(blk):
        v = blk.astype(F32)
        mid = v - jnp.mean(v, -1, keepdims=True)
        rs = lax.rsqrt(jnp.mean(mid * mid, -1, keepdims=True) + EPSILON)
        return mid * rs, rs

    def norm_back(e, n, rs, gain, row):
        sgv[row : row + 1, :] += jnp.sum(e * n, 0, keepdims=True)
        sgv[row + 1 : row + 2, :] += jnp.sum(e, 0, keepdims=True)
        eg = e * gain
        return rs * (
            eg - jnp.mean(eg, -1, keepdims=True) - n * jnp.mean(eg * n, -1, keepdims=True)
        )

    def feed(n2t, hidt, gup, gst):
        def gsum(b, carry):
            at = pl.ds(mult((2 * c + y) * R + b * TT, TT), TT)
            sgv[4:5, :] += jnp.sum(G4[at, :].astype(F32), 0, keepdims=True)
            return carry

        lax.fori_loop(0, R // TT, gsum, 0)
        bias = jnp.concatenate(
            [
                jnp.where(
                    y == 0,
                    vecs[8 + rr : 9 + rr, ds(2 * xx + c, RS)],
                    vecs[10 + rr : 11 + rr, ds(2 * xx + c, RS)],
                )
                for xx in range(X)
                for rr in range(2)
            ],
            1,
        )
        for u in range(4):
            gather_fwd(u)
            if u + 2 < len(units):
                gather_x(u + 2)
        gather_wait(0)
        gather_wait(1)
        half_tiles = T // TT // 2

        def tile(i, gb):
            @pl.when(i == half_tiles - 1)
            def _():
                exchange_forward()

            @pl.when(i == half_tiles)
            def _():
                exchange_finish()

            yy = jnp.where(i < half_tiles, y, yo)
            j = lax.rem(i, half_tiles)
            per = R // TT
            rows = pl.ds(mult((2 * lax.div(j, per) + yy) * R + lax.rem(j, per) * TT, TT), TT)
            n, rs = center(X4[rows, :])
            n2 = (n * vec(2) + vec(3)).astype(BF)
            n2t[:, rows] = n2.T
            up = mm(n2, wup[...]) + bias
            cdf = 0.5 + 0.5 * lax.erf(up * (1.0 / math.sqrt(2.0)))
            hd = (up * cdf).astype(BF)
            hidt[:, rows] = hd.T
            gh = mm(G4[rows, :], wdn[...], NT)
            pdf = jnp.exp(-0.5 * up * up) * (1.0 / math.sqrt(2.0 * math.pi))
            gu = (gh * (cdf + up * pdf)).astype(BF)
            gup[rows, :] = gu
            OB[rows, :] = mm(hd, wdn[...]).astype(BF)
            gn = mm(gu, wup[...], NT)
            TB[rows, :] = norm_back(gn, n, rs, vec(2), 2).astype(BF)
            return gb + jnp.sum(gu.astype(F32), 0, keepdims=True)

        gb = lax.fori_loop(0, T // TT, tile, jnp.zeros((1, FL), F32))
        for yy in range(2):

            @pl.when(y == yy)
            def _():
                for xx in range(X):
                    for rr in range(2):
                        at = (2 * xx + rr) * RS
                        row = 5 + 2 * yy + rr
                        sgv[row : row + 1, ds(2 * xx + c, RS)] = gb[:, at : at + RS]

        gather_fwd(4)
        gather_fwd(5)
        for t in range(NU):
            grad_piece(t, n2t, lambda: gup[:, t * PW : (t + 1) * PW], gst)
        for t in range(NU):
            tick(1)
            grad_piece(NU + t, hidt, lambda: G4[:, t * PW : (t + 1) * PW], gst)
        flush()

    pl.run_scoped(
        feed,
        pltpu.VMEM((D, T), BF),
        pltpu.VMEM((FL, T), BF),
        pltpu.VMEM((T, FL), BF),
        pltpu.VMEM((2, X, RX, PW), BF),
    )

    s_mo = [S() for _ in range(2)]
    r_mo = [S() for _ in range(2)]
    s_af = [S() for _ in range(2)]
    r_af = [S() for _ in range(2)]
    l_tab, l_st, l_fin = S(), S(), S()
    s_sga, r_sga, l_sga = S(), S(), S()
    s_sgb, r_sgb, l_sgb = S(), S(), S()

    def give(a, buf, cc):
        @pl.when(c != cc)
        def _():
            rcopy(buf.at[pl.ds(cc * L, L)], mo.at[a], s_mo[a], r_mo[a], fsdp=fs)

    def take(a, buf, room, cc):
        @pl.when(c == cc)
        def _():
            wait(r_mo[a], mo.at[a])
            lcopy(mo.at[a], room.at[pl.ds(0, L)], l_st).wait()

            def add(i, carry):
                rows = pl.ds(mult(cc * L + i * 64, 64), 64)
                buf[rows, :] = (buf[rows, :].astype(F32) + room[ds(i, 64), :].astype(F32)).astype(
                    BF
                )
                return carry

            lax.fori_loop(0, L // 64, add, 0)
            rcopy(buf.at[ds(2 * cc + yo, R)], af.at[a], s_af[a], r_af[a], ctx=yo)

    def last(a, buf, room, dst):
        wait(r_af[a], af.at[a])
        lcopy(af.at[a], room.at[pl.ds(0, R)], l_st).wait()

        def add(i, carry):
            rows = pl.ds(mult((2 * c + y) * R + i * 64, 64), 64)
            total = buf[rows, :].astype(F32) + room[ds(i, 64), :].astype(F32)
            if a == 0:
                total = total + X4[rows, :].astype(F32) + vec(7) + vec(12)
            else:
                total = total + G4[rows, :].astype(F32)
            room[ds(i, 64), :] = total.astype(BF)
            return carry

        lax.fori_loop(0, R // 64, add, 0)
        lcopy(room.at[pl.ds(0, R)], dst, l_fin)

    def attend(n1t, ga, qkv, ctx, ctxt, gctx, gproj, dkv, tab, gst):
        lcopy(tab_ref, tab, l_tab)
        wait(l_oh, oh_ref)
        wait(r_oh, oh_ref)

        def weight(cc, b, s, width):
            w = oh_v[cc, pl.ds(b * NB + s, 1), :].astype(BF)
            return jnp.concatenate([w] * (width // 128), 1)

        def in_order(ref, cc, b):
            total = None
            for s in range(NB):
                rows = pl.ds(mult(cc * L + s * TT, TT), TT)
                term = ref[rows, :] * weight(cc, b, s, D)
                total = term if total is None else total + term
            return total

        def in_slot(ref, cc, s, width):
            total = None
            for b in range(NB):
                rows = pl.ds(mult(cc * L + b * TT, TT), TT)
                term = ref[rows, :] * weight(cc, b, s, width)
                total = term if total is None else total + term
            return total

        def turned(v, rows, sign):
            right = pltpu.roll(v, ROT // 2, 1)
            left = pltpu.roll(v, 128 - ROT // 2, 1)
            return v * tab[0, rows, :] + sign * (
                right * tab[1, rows, :] + left * tab[2, rows, :]
            )

        def pick(options):
            a = jnp.where(c == 0, options[0], options[2])
            b = jnp.where(c == 0, options[1], options[3])
            return jnp.where(y == 0, a, b)

        def spot(m, xx, cc, yy):
            e = D * m + (D // X) * xx + (D // (2 * X)) * cc + HX * yy
            rest = e % (3 * RS)
            return e // (3 * RS), rest // RS, rest % RS

        bias = jnp.concatenate(
            [
                pick(
                    [
                        jnp.concatenate(
                            [
                                sm_v[ff, 4 + row : 5 + row, lane : lane + HX]
                                for ff, row, lane in [spot(m, xx, cc, yy) for xx in range(X)]
                            ],
                            1,
                        )
                        for cc in range(2)
                        for yy in range(2)
                    ]
                )
                for m in range(3)
            ],
            1,
        )
        wait(l_tab, tab_ref)
        gather_wait(2)
        gather_wait(3)

        def prep(t, carry):
            cc, b = lax.div(t, NB), lax.rem(t, NB)
            n, _ = center(in_order(X4, cc, b))
            n1 = (n * vec(0) + vec(1)).astype(BF)
            n1t[:, ds(t)] = n1.T
            gv = in_order(G4, cc, b)
            ga[ds(t), :] = gv
            v = mm(n1, wqkv[...]) + bias
            for m in range(2):
                for u in range(HC // 128):
                    w = turned(v[:, m * HC + u * 128 : m * HC + (u + 1) * 128], ds(b), 1.0)
                    if m == 0:
                        w = w * (1.0 / math.sqrt(HEAD))
                    qkv[m, ds(t), u * 128 : (u + 1) * 128] = w.astype(BF)
            qkv[2, ds(t), :] = v[:, 2 * HC :].astype(BF)
            gctx[ds(t), :] = mm(gv, wo[...], NT).astype(BF)
            return carry

        lax.fori_loop(0, T // TT, prep, 0)
        tick(1)

        low_half = lax.broadcasted_iota(jnp.int32, (1, 128), 1) < HEAD
        dkv[...] = jnp.zeros_like(dkv)
        pairs = HC // 128
        for u in range(4):
            wait(gzs[u], xz_bytes(u // 2))
        for cc in range(2):
            for i in range(NB):
                n = (i + 1) * TT

                def pair(hp, carry):
                    lanes = pl.ds(mult(hp * 128, 128), 128)
                    rows = pl.ds(cc * L + i * TT, TT)
                    seen = pl.ds(cc * L, n)
                    qb = qkv[0, rows, lanes]
                    gb = gctx[rows, lanes]
                    kb = qkv[1, seen, lanes]
                    vb = qkv[2, seen, lanes]
                    ahead = lax.broadcasted_iota(jnp.int32, (TT, n), 1) - lax.broadcasted_iota(
                        jnp.int32, (TT, n), 0
                    )
                    zero = jnp.zeros_like(qb)
                    res = []
                    for hd in range(2):
                        mask = low_half if hd == 0 else jnp.logical_not(low_half)
                        s = mm(jnp.where(mask, qb, zero), kb, NT)
                        s = jnp.where(ahead <= i * TT, s, -1e30)
                        p = jnp.exp(s - jnp.max(s, -1, keepdims=True))
                        p = p * (1.0 / jnp.sum(p, -1, keepdims=True))
                        pb = p.astype(BF)
                        dp = mm(jnp.where(mask, gb, zero), vb, NT)
                        dsc = (p * (dp - jnp.sum(p * dp, -1, keepdims=True))).astype(BF)
                        res.append((mm(pb, vb), mm(dsc, kb), mm(dsc, qb, TN), mm(pb, gb, TN)))
                    both = [jnp.where(low_half, u0, u1) for u0, u1 in zip(res[0], res[1])]
                    cb = both[0].astype(BF)
                    ctx[rows, lanes] = cb
                    ctxt[lanes, rows] = cb.T
                    dq = turned(both[1] * (1.0 / math.sqrt(HEAD)), pl.ds(i * TT, TT), -1.0)
                    gproj[rows, lanes] = dq.astype(BF)
                    dkv[0, seen, lanes] += both[2]
                    dkv[1, seen, lanes] += both[3]
                    return carry

                lax.fori_loop(0, pairs, pair, 0)
                tick(1)
                if cc == 1 and i == 1:
                    take(0, OB, wup, 0)
                    take(1, TB, wdn, 0)

            if cc == 1:
                grad_piece(2 * NU, ctxt, lambda: ga[...], gst)
                grad_piece(2 * NU + 1, n1t, lambda: gproj[:, 0:HC], gst)

            def turn_back(b, carry):
                t = cc * NB + b
                for u in range(pairs):
                    at = pl.ds(u * 128, 128)
                    gproj[ds(t), HC + u * 128 : HC + (u + 1) * 128] = turned(
                        dkv[0, ds(t), at], ds(b), -1.0
                    ).astype(BF)
                gproj[ds(t), 2 * HC : 3 * HC] = dkv[1, ds(t), :].astype(BF)
                return carry

            lax.fori_loop(0, NB, turn_back, 0)
            if cc == 1:
                for m in (2, 1):
                    grad_piece(2 * NU + 1 + m, n1t, lambda: gproj[:, m * HC : (m + 1) * HC], gst)
                flush()

            def att_out(s, carry):
                t = cc * NB + s
                a = mm(in_slot(ctx, cc, s, HC), wo[...])
                OB[ds(t), :] = (OB[ds(t), :].astype(F32) + a).astype(BF)
                return carry

            lax.fori_loop(0, NB, att_out, 0)
            give(0, OB, cc)
            if cc == 1:
                tick(1)

            def att_in(s, carry):
                t = cc * NB + s
                e = mm(in_slot(gproj, cc, s, 3 * HC), wqkv[...], NT)
                n, rs = center(X4[ds(t), :])
                term = norm_back(e, n, rs, vec(0), 0)
                TB[ds(t), :] = (TB[ds(t), :].astype(F32) + term).astype(BF)
                return carry

            lax.fori_loop(0, NB, att_in, 0)
            give(1, TB, cc)
            if cc == 1:
                take(0, OB, wup, 1)
                tick(1)

        for m in range(3):
            gb = jnp.sum(gproj[:, m * HC : (m + 1) * HC].astype(F32), 0, keepdims=True)
            for cc in range(2):
                for yy in range(2):

                    @pl.when((c == cc) & (y == yy))
                    def _():
                        for xx in range(X):
                            ff, row, lane = spot(m, xx, cc, yy)
                            at = ff * RS + lane
                            sgv[9 + row : 10 + row, at : at + HX] = gb[:, xx * HX : (xx + 1) * HX]

    pl.run_scoped(
        attend,
        pltpu.VMEM((D, T), BF),
        pltpu.VMEM((T, D), BF),
        pltpu.VMEM((3, T, HC), BF),
        pltpu.VMEM((T, HC), BF),
        pltpu.VMEM((HC, T), BF),
        pltpu.VMEM((T, HC), BF),
        pltpu.VMEM((T, 3 * HC), BF),
        pltpu.VMEM((2, T, HC), F32),
        pltpu.VMEM((3, L, 128), F32),
        pltpu.VMEM((2, X, RX, PW), BF),
    )

    here = f * 2 + y
    lcopy(sgv, sgA.at[here], l_sga)
    for dev in near[: 4 * X - 1]:
        rcopy(sgv, sgA.at[here], s_sga, r_sga, **dev)
    tick(1)
    take(1, TB, wdn, 1)
    tick(1)
    wait(l_sga, sgv)
    wait(r_sga, sgA.at[pl.ds(0, 4 * X - 1)])
    total = sgA[0]
    for i in range(1, 4 * X):
        total = total + sgA[i]
    wait(s_sga, sgA.at[pl.ds(0, 4 * X - 1)])
    sgv[...] = total
    lcopy(sgv, sgB.at[r], l_sgb)
    for dev in near[4 * X - 1 :]:
        rcopy(sgv, sgB.at[r], s_sgb, r_sgb, **dev)
    tick(1)
    tick(1, True)
    last(0, OB, wup, out_ref)
    wait(l_sgb, sgv)
    wait(r_sgb, sgB.at[pl.ds(0, NREP - 1)])
    wait(s_sgb, sgB.at[pl.ds(0, NREP - 1)])
    total = sgB[0]
    for i in range(1, NREP):
        total = total + sgB[i]
    sgv[...] = total
    lcopy(sgv, sg_ref, l_sga)
    while live or moving or ready:
        tick(1, True)
    last(1, TB, wdn, gin_ref)

    wait(l_sga, sgv)
    wait(l_fin, af)
    for a in range(2):
        wait(s_mo[a], mo.at[a])
        wait(s_af[a], af.at[a])
    wait(s_sm, sm_v.at[pl.ds(0, 2 * X - 1)])
    wait(s_oh, oh_ref)
    for src, dst, ids in tok:
        for k in (1, 3, 5):
            wait(ids[k], src)
    for fn in finals:
        fn()

    @pl.when(depth > 0)
    def _():
        for p in range(NP):
            wait(zbs[p], own.at[0])


def sem_count(NP):
    return 4 * 6 + 3 * 4 + 9 * NP + 64


def body(
    residual_in,
    block_order,
    ln1_gain,
    ln1_bias,
    ln2_gain,
    ln2_bias,
    w_qkv,
    b_qkv,
    w_out,
    b_out,
    w_up,
    b_up,
    w_down,
    b_down,
    cotangent,
):
    R, D = residual_in.shape[1:]
    FF = w_up.shape[1]
    NF = lax.axis_size("fsdp")
    NREP = lax.axis_size("rep")
    X = NF // 2
    L, T, RX, RS = 2 * R, 4 * R, D // X, D // NF
    FL, HC = FF // 4, D // 4
    HX = HC // X
    NP = 2 * (FL // PW) + 4
    f = lax.axis_index("fsdp")

    order = block_order[0]
    count = order.shape[0]
    spots = jnp.arange(count, dtype=jnp.int32)
    where = (order[None, :] == spots[:, None]).astype(F32).reshape(-1, 1)
    where = jnp.broadcast_to(where, (count * count, 128))
    small, at = None, 0
    for v in (ln1_gain, ln1_bias, ln2_gain, ln2_bias, b_qkv, b_out, b_up, b_down):
        n = v.shape[0]
        term = jnp.pad(v.astype(F32), (at, 16 * RS - at - n))
        small = term if small is None else small + term
        at += n
    small = small.reshape(16, RS)
    halves = ROT // 2
    lane = np.arange(128) % HEAD
    angles = np.arange(L)[:, None] * 10000.0 ** (-2.0 * (lane % halves) / ROT)[None, :]
    cosine, sine = np.cos(angles), np.sin(angles)
    tab = np.stack(
        [
            np.where(lane < ROT, cosine, 1.0),
            np.where((lane < ROT) & (lane >= halves), sine, 0.0),
            np.where(lane < halves, -sine, 0.0),
        ]
    ).astype(np.float32)

    def columns(w):
        if HX >= 128:
            return w
        w = w.reshape(RS, 3, X, 2, 2, HX).transpose(0, 3, 4, 1, 2, 5)
        return w.reshape(RS, 3 * D)

    def columns_back(w):
        if HX >= 128:
            return w
        w = w.reshape(RS, 2, 2, 3, X, HX).transpose(0, 3, 4, 1, 2, 5)
        return w.reshape(RS, 3 * D)

    anywhere = pl.BlockSpec(memory_space=pl.ANY)
    sds = jax.ShapeDtypeStruct
    outs = pl.pallas_call(
        functools.partial(kernel, (X, NREP, R, D, FF)),
        out_shape=(
            sds((RS, FF), BF),
            sds((FF // NF, D), BF),
            sds((RS, 3 * D), BF),
            sds((RS, D), BF),
            sds((R, D), BF),
            sds((R, D), BF),
            sds((16, D), F32),
            sds((NP, X, RX, PW), BF),
            sds((2, L, D), BF),
            sds((2, R, D), BF),
        ),
        in_specs=[anywhere] * 9,
        out_specs=(anywhere,) * 10,
        scratch_shapes=[
            pltpu.VMEM((T, D), BF),
            pltpu.VMEM((T, D), BF),
            pltpu.VMEM((D, FL), BF),
            pltpu.VMEM((FL, D), BF),
            pltpu.VMEM((D, 3 * HC), BF),
            pltpu.VMEM((HC, D), BF),
            pltpu.VMEM((2, (L // TT) ** 2, 128), F32),
            pltpu.VMEM((NF, 16, RS), F32),
            pltpu.VMEM((16, D), F32),
            pltpu.VMEM((16, D), F32),
            pltpu.VMEM((2 * NF, 16, D), F32),
            pltpu.VMEM((NREP, 16, D), F32),
            pltpu.VMEM((NP, RX, PW), BF),
            pltpu.VMEM((NP, RX, PW), BF),
            pltpu.VMEM((NP, RX, PW), BF),
            pltpu.VMEM((NP, X - 1, RX, PW), BF),
            pltpu.VMEM((T, D), BF),
            pltpu.VMEM((T, D), BF),
            pltpu.SemaphoreType.DMA((sem_count(NP),)),
        ],
        compiler_params=pltpu.CompilerParams(
            collective_id=0, has_side_effects=True, vmem_limit_bytes=63 * 1024 * 1024
        ),
    )(
        residual_in.reshape(R, D),
        cotangent.reshape(R, D),
        where,
        small,
        columns(w_qkv),
        w_out,
        w_up,
        w_down,
        tab,
    )
    fin_up, fin_dn, fin_qkv, fin_o, out, gin, sg = outs[:7]
    mine = lax.dynamic_slice(sg, (0, f * RS), (16, RS))
    return (
        out[None],
        gin.astype(F32)[None],
        mine[0],
        mine[1],
        mine[2],
        mine[3],
        columns_back(fin_qkv).astype(F32),
        mine[9:12].reshape(-1),
        fin_o.astype(F32),
        mine[4],
        fin_up.astype(F32),
        mine[5:9].reshape(-1),
        fin_dn.astype(F32),
        mine[4],
    )


def solution(mesh):
    in_specs = (
        P(("rep", "fsdp"), "ctx", None),
        P(("rep", "fsdp"), None),
        P("fsdp"),
        P("fsdp"),
        P("fsdp"),
        P("fsdp"),
        P("fsdp", None),
        P("fsdp"),
        P("fsdp", None),
        P("fsdp"),
        P("fsdp", None),
        P("fsdp"),
        P("fsdp", None),
        P("fsdp"),
        P(("rep", "fsdp"), "ctx", None),
    )
    out_specs = (
        P(("rep", "fsdp"), "ctx", None),
        P(("rep", "fsdp"), "ctx", None),
        P("fsdp"),
        P("fsdp"),
        P("fsdp"),
        P("fsdp"),
        P("fsdp", None),
        P("fsdp"),
        P("fsdp", None),
        P("fsdp"),
        P("fsdp", None),
        P("fsdp"),
        P("fsdp", None),
        P("fsdp"),
    )
    return jax.shard_map(body, mesh=mesh, in_specs=in_specs, out_specs=out_specs, check_vma=False)
```
